256 devices in a mesh: grp: 8 (over x, z_lo), lat: 32 (over y, z_hi, core).
Axes of the slice: x: 4, y: 4, z: 8 (z_hi: 4, z_lo: 2; z = z_hi * 2 + z_lo), core: 2. Of those that a mesh axis runs over, the one named last changes fastest.
Arguments:
- inputs: bfloat16 [512, 8192], P('lat'), may hold values from -6 to 6
- dec_bias: float32 [8192], replicated, may hold values from -3 to 3
- weight: bfloat16 [32768, 8192], P(('grp', 'lat')), may hold values from -0.0625 to 0.0625
- enc_bias: float32 [32768], P(('grp', 'lat')), may hold values from -1 to 0.5
- first_moment: bfloat16 [32768, 8192], P(('grp', 'lat')), may hold values from -0.15625 to 0.15625
- second_moment: bfloat16 [32768, 8192], P(('grp', 'lat')), may hold values from 9.953976e-06 to 0.0009994507
Outputs:
- update: bfloat16 [32768, 8192], P(('grp', 'lat'))
- new_first: bfloat16 [32768, 8192], P(('grp', 'lat'))
- new_second: bfloat16 [32768, 8192], P(('grp', 'lat'))
The draws below stay inside these ranges and needn't reach their ends.
All inputs are finite; a program needn't handle non-finite values.
Results may differ from the reference program's by a relative error of at most 0.014.
The reference program's roundings to bfloat16 on the way (of `centered`, `activity`, `error` and `pre_grad`) count: a program that leaves them out, or rounds other values in their place, can miss the bound.
Values may be sent and summed in bfloat16 or wider, within the bound.
No kernel may reach another device: no remote copies, remote signals or barrier semaphores. Data moves between devices by JAX's collectives and lax.ppermute only.
A program may use at most 128 MiB of HBM per device.

```python
import math
import jax
import jax.numpy as jnp

D = 8192
STEP = 100
LATENTS = 32768
ROWS = 512


def shard_levels(stream_key, dims, cuts, smallest, high):
    factor_of, own = 1.0, jax.random.fold_in(stream_key, 6)
    for position, parts in cuts:
        steps = jnp.exp(jax.random.uniform(jax.random.fold_in(own, position), (parts,), jnp.float32, smallest / len(cuts), high / len(cuts)))
        factor_of = factor_of * jnp.repeat(steps, dims[position] // parts).reshape([-1 if axis == position else 1 for axis in range(len(dims))])
    return factor_of


def normal_values(own_key, dims, scale, most, split=(), held_as=jnp.bfloat16):
    result = jax.random.normal(own_key, dims, jnp.float32) * scale
    if len(split) > 0:
        result = shard_levels(own_key, dims, split, -0.22, 0.18) * result
    return jnp.clip(result, min=-most, max=most).astype(held_as)


def setup_inputs(seed: int = 0) -> dict:
    arg_keys = jax.random.split(jax.random.key(seed), 7)
    inputs = normal_values(arg_keys[0], (ROWS, D), 1.0, 6.0, ((0, 32),))
    dec_bias = normal_values(arg_keys[1], (D,), 0.5, 3.0, (), jnp.float32)
    weight = normal_values(arg_keys[2], (LATENTS, D), D ** -0.5, 0.0625, ((0, 256),))
    enc_bias = jnp.clip(-1.0 + 1.5 * jax.random.uniform(arg_keys[3], (LATENTS,), jnp.float32) ** shard_levels(arg_keys[3], (LATENTS,), ((0, 256),), -0.2, 0.2), -1.0, 0.5)
    first_moment = normal_values(arg_keys[4], (LATENTS, D), 0.01, 0.15625, ((0, 256),))
    second_moment = jnp.clip(jnp.exp(math.log(0.0009994507) - 4.609234 * jax.random.uniform(arg_keys[5], (LATENTS, D), jnp.float32) ** shard_levels(arg_keys[5], (LATENTS, D), ((0, 256),), -0.2, 0.2)), 9.953975677490234e-06, 0.0009994507).astype(jnp.bfloat16)
    return dict(inputs=inputs, dec_bias=dec_bias, weight=weight, enc_bias=enc_bias, first_moment=first_moment, second_moment=second_moment)


def reference(inputs, dec_bias, weight, enc_bias, first_moment, second_moment):
    source = inputs.astype(jnp.float32)
    centered = (source - dec_bias).astype(jnp.bfloat16)
    preact = jnp.dot(centered, weight.T, preferred_element_type=jnp.float32) + enc_bias
    activity = jnp.maximum(preact, 0.0).astype(jnp.bfloat16)
    recon = jnp.dot(activity, weight, preferred_element_type=jnp.float32)
    error = (recon + dec_bias - source).astype(jnp.bfloat16)
    back = jnp.dot(error, weight.T, preferred_element_type=jnp.float32)
    pre_grad = jnp.where(preact > 0, back, 0.0).astype(jnp.bfloat16)
    grad_sum = jnp.dot(activity.T, error, preferred_element_type=jnp.float32) + jnp.dot(pre_grad.T, centered, preferred_element_type=jnp.float32)
    gradient = grad_sum / ROWS
    first = 0.9 * first_moment.astype(jnp.float32) + 0.1 * gradient
    second = 0.999 * second_moment.astype(jnp.float32) + 0.001 * gradient * gradient
    update = first / (1.0 - 0.9 ** STEP) / (jnp.sqrt(second / (1.0 - 0.999 ** STEP)) + 1e-08)
    return (update.astype(jnp.bfloat16), first.astype(jnp.bfloat16), second.astype(jnp.bfloat16))
```

```python
import jax
import jax.numpy as jnp
from jax import lax
from jax.sharding import Mesh, PartitionSpec as P

STEP = 100
BF16 = jnp.bfloat16
F32 = jnp.float32
Z = ("zh", "zl")
LAST = (((1,), (1,)), ((), ()))
FIRST = (((0,), (0,)), ((), ()))


def shift(value, axis, by):
    size = lax.axis_size(axis)
    return lax.ppermute(value, axis, [(i, (i + by) % size) for i in range(size)])


def swap(value):
    return lax.ppermute(value, "c", [(0, 1), (1, 0)])


def spread(piece, axis):
    size = lax.axis_size(axis)
    me = lax.axis_index(axis)
    found = [(me, piece)]
    for by in (2, 1, 3):
        found.append(((me - by) % size, shift(piece, axis, by)))
    return found


def collect(block_of, axis):
    size = lax.axis_size(axis)
    me = lax.axis_index(axis)
    total = None
    for by in (2, 1, 3):
        arrived = shift(block_of((me + by) % size), axis, by).astype(F32)
        total = arrived if total is None else total + arrived
    return total + block_of(me).astype(F32)


def lay(found, dim):
    size = found[0][1].shape[dim]
    shape = list(found[0][1].shape)
    shape[dim] = size * len(found)
    full = jnp.zeros(shape, found[0][1].dtype)
    for place, piece in found:
        full = lax.dynamic_update_slice_in_dim(full, piece, place * size, dim)
    return full


def gather_inputs(rows):
    x = lax.axis_index("x")
    width = rows.shape[1] // 2
    part = width // 4
    left = lax.dynamic_slice_in_dim(rows, x * part, part, 1)
    right = lax.dynamic_slice_in_dim(rows, width + x * part, part, 1)
    both = lay(spread(jnp.concatenate([left, right], 1), "zh"), 0)
    left, right = both[:, :part], both[:, part:]
    left = lay(spread(left, "y"), 0)
    right = lay(spread(right, "x"), 1)
    left = spread(left, "x")
    right = spread(right, "y")
    return jnp.concatenate([lay(left, 1), lay(right, 0)], 1)


def body(inputs, dec_bias, weight, enc_bias, first_moment, second_moment):
    latents, width = weight.shape
    half = width // 2
    part = half // 4
    x, y = lax.axis_index("x"), lax.axis_index("y")
    z = lax.axis_index(Z)

    pair = jnp.concatenate([weight, swap(weight)], 0)
    pair_bias = jnp.concatenate([enc_bias, swap(enc_bias)], 0)

    source = gather_inputs(inputs)
    rows = source.shape[0]
    centered = (source.astype(F32) - dec_bias).astype(BF16)
    preact = lax.dot_general(centered, pair, LAST, preferred_element_type=F32) + pair_bias
    activity = jnp.maximum(preact, 0.0).astype(BF16)

    def recon_block(first_column):
        columns = lax.dynamic_slice_in_dim(pair, first_column, part, 1)
        return jnp.dot(activity, columns, preferred_element_type=F32).astype(BF16)

    left = collect(lambda b: recon_block(b * part), "x").astype(BF16)
    right = collect(lambda b: recon_block(half + b * part), "y").astype(BF16)
    strip = rows // 4
    left = collect(lambda b: lax.dynamic_slice_in_dim(left, b * strip, strip, 0), "y").astype(BF16)
    right = collect(lambda b: lax.dynamic_slice_in_dim(right, b * strip, strip, 0), "x").astype(BF16)
    thin = strip // 8
    both = jnp.concatenate([left.reshape(8, thin, part), right.reshape(8, thin, part)], 1)
    both = lax.all_to_all(both, Z, 0, 0, tiled=True)
    recon = jnp.sum(both.astype(F32), 0)

    def own(array, row, column):
        return lax.dynamic_slice(array, (row, column), (thin, part)).astype(F32)

    left_column, right_column = x * part, half + y * part
    left_source = own(source, y * strip + z * thin, left_column)
    right_source = own(source, x * strip + z * thin, right_column)
    bias = jnp.concatenate(
        [
            jnp.broadcast_to(lax.dynamic_slice_in_dim(dec_bias, left_column, part, 0), (thin, part)),
            jnp.broadcast_to(lax.dynamic_slice_in_dim(dec_bias, right_column, part, 0), (thin, part)),
        ],
        0,
    )
    error = (recon + bias - jnp.concatenate([left_source, right_source], 0)).astype(BF16)

    both = lax.all_to_all(jnp.broadcast_to(error, (8, 2 * thin, part)), Z, 0, 0, tiled=True)
    left, right = both[:, :thin].reshape(strip, part), both[:, thin:].reshape(strip, part)
    left = lay(spread(left, "y"), 0)
    right = lay(spread(right, "x"), 0)
    error = jnp.concatenate([lay(spread(left, "x"), 1), lay(spread(right, "y"), 1)], 1)

    back = lax.dot_general(error, pair, LAST, preferred_element_type=F32)
    pre_grad = jnp.where(preact > 0, back, 0.0).astype(BF16)
    coded = jnp.concatenate([activity, pre_grad], 0)
    seen = jnp.concatenate([error, centered], 0)

    theirs = lax.dot_general(coded[:, latents:], seen, FIRST, preferred_element_type=F32).astype(BF16)
    theirs = swap(theirs)
    mine = lax.dot_general(coded[:, :latents], seen, FIRST, preferred_element_type=F32)
    gradient = (mine + theirs.astype(F32)) / (rows * 2)
    first = 0.9 * first_moment.astype(F32) + 0.1 * gradient
    second = 0.999 * second_moment.astype(F32) + 0.001 * gradient * gradient
    update = first / (1.0 - 0.9**STEP) / (jnp.sqrt(second / (1.0 - 0.999**STEP)) + 1e-08)
    return (update.astype(BF16), first.astype(BF16), second.astype(BF16))


def solution(mesh):
    fine = Mesh(mesh.devices.reshape(4, 2, 4, 4, 2), ("x", "zl", "y", "zh", "c"))
    lat = ("y", "zh", "c")
    everything = ("x", "zl", "y", "zh", "c")
    return jax.shard_map(
        body,
        mesh=fine,
        in_specs=(P(lat, None), P(), P(everything, None), P(everything), P(everything, None), P(everything, None)),
        out_specs=(P(everything, None),) * 3,
        check_vma=False,
    )
```

```python
import functools

import jax
import jax.numpy as jnp
from jax import lax
from jax.experimental import pallas as pl
from jax.experimental.pallas import tpu as pltpu
from jax.sharding import Mesh, PartitionSpec as P

STEP = 100
BF16 = jnp.bfloat16
F32 = jnp.float32
SIDE = 4
ORDER = (0, 2, 1, 3)
PLANE = ("x", "y", "c")
Z = ("zh", "zl")
VMEM = pl.BlockSpec(memory_space=pltpu.VMEM)
SMEM = pl.BlockSpec(memory_space=pltpu.SMEM)
PARAMS = pltpu.CompilerParams(vmem_limit_bytes=48 * 1024 * 1024)


def plane_pairs(by, last):
    pairs = []
    for x in range(SIDE):
        for y in range(SIDE):
            for c in range(2):
                along_x = (c == 0) == last
                to_x = (x + by) % SIDE if along_x else x
                to_y = y if along_x else (y + by) % SIDE
                pairs.append(((x * SIDE + y) * 2 + c, (to_x * SIDE + to_y) * 2 + c))
    return pairs


def shift(value, by, last):
    return lax.ppermute(value, PLANE, plane_pairs(by, last))


def swap(value):
    return lax.ppermute(value, "c", [(0, 1), (1, 0)])


def spread(piece, last):
    return [piece] + [shift(piece, by, last) for by in ORDER[1:]]


def call(kernel, out_shape, args, flops, specs=None, params=PARAMS):
    shapes = jax.tree.leaves(out_shape)
    moved = sum(a.size * a.dtype.itemsize for a in list(args) + shapes)
    return pl.pallas_call(
        kernel,
        out_shape=out_shape,
        in_specs=specs or [VMEM] * len(args),
        out_specs=jax.tree.map(lambda _: VMEM, out_shape),
        compiler_params=params,
        cost_estimate=pl.CostEstimate(flops=flops, bytes_accessed=moved, transcendentals=0),
    )(*args)


def project_kernel(place, weight, extra, *refs, centre):
    pieces, (laid, product) = refs[:4], refs[4:]
    thick, part = pieces[0].shape[1:]
    product[...] = jnp.zeros_like(product)
    for i, piece in enumerate(pieces):

        def step(j, carry, i=i, piece=piece):
            row = pl.multiple_of(place[0, i * SIDE + j] * thick, thick)
            column = pl.multiple_of(place[1, i * SIDE + j] * part, part)
            block = piece[j]
            if centre:
                block = (block.astype(F32) - extra[:, pl.ds(column, part)]).astype(BF16)
            laid[pl.ds(row, thick), pl.ds(column, part)] = block
            product[pl.ds(row, thick), :] += lax.dot_general(
                block,
                weight[:, pl.ds(column, part)],
                (((1,), (1,)), ((), ())),
                preferred_element_type=F32,
            )
            return carry

        lax.fori_loop(0, SIDE, step, 0)


def project(place, weight, extra, pieces, centre):
    thick, part = pieces[0].shape[1:]
    rows, width = thick * SIDE, part * SIDE
    return call(
        functools.partial(project_kernel, centre=centre),
        (jax.ShapeDtypeStruct((rows, width), BF16), jax.ShapeDtypeStruct((rows, weight.shape[0]), F32)),
        (place, weight, extra, *pieces),
        2 * rows * width * weight.shape[0],
        [SMEM] + [VMEM] * (2 + SIDE),
    )


def join(own, other, latents):
    return jnp.concatenate([own[:, :latents] + other[:, latents:], own[:, latents:] + other[:, :latents]], 1)


def activate_kernel(own, other, bias, preact, activity, flat):
    latents = bias.shape[1] // 2
    value = join(own[...], other[...], latents) + bias[...]
    preact[...] = value
    positive = jnp.maximum(value, 0.0)
    activity[...] = positive.astype(BF16)
    flat[...] = positive.T.astype(BF16)


def recon_kernel(place, activity, weight, block, *, slot):
    _, thick, part = block.shape

    def step(j, carry):
        row = pl.multiple_of(place[0, slot * SIDE + j] * thick, thick)
        column = pl.multiple_of(place[1, slot * SIDE + j] * part, part)
        block[j] = jnp.dot(
            activity[pl.ds(row, thick), :], weight[:, pl.ds(column, part)], preferred_element_type=F32
        ).astype(BF16)
        return carry

    lax.fori_loop(0, SIDE, step, 0)


def gradient_kernel(own, other, preact, flat, error, centered, mine, theirs, slope, *, chunk):
    latents = mine.shape[0]
    value = jnp.where(preact[...] > 0, join(own[...], other[...], latents), 0.0)
    slope[...] = value.T.astype(BF16)

    def step(j, carry):
        columns = pl.ds(pl.multiple_of(j * chunk, chunk), chunk)
        total = jnp.dot(flat[...], error[:, columns], preferred_element_type=F32)
        total += jnp.dot(slope[...], centered[:, columns], preferred_element_type=F32)
        mine[:, columns] = total[:latents]
        theirs[:, columns] = total[latents:].astype(BF16)
        return carry

    lax.fori_loop(0, mine.shape[1] // chunk, step, 0)


def adam_kernel(at, gradient_ref, first_ref, second_ref, *refs, rows):
    update_out, first_out, second_out = refs[-3:]
    gradient = gradient_ref[...].astype(F32) * (1.0 / rows)
    first = 0.9 * first_ref[...].astype(F32) + 0.1 * gradient
    second = 0.999 * second_ref[...].astype(F32) + 0.001 * gradient * gradient
    update = first * (1.0 / (1.0 - 0.9**STEP)) / (jnp.sqrt(second * (1.0 / (1.0 - 0.999**STEP))) + 1e-08)
    update_out[...] = update.astype(BF16)
    first_out[...] = first.astype(BF16)
    second_out[...] = second.astype(BF16)


def adam(at, gradient, first_moment, second_moment, outs, rows, chunk=512):
    latents, width = gradient.shape
    count = width // chunk
    here = pl.BlockSpec((latents, chunk), lambda i, at: (0, i))
    there = pl.BlockSpec((latents, chunk), lambda i, at: (0, at[0] * count + i))
    held = [pl.BlockSpec(memory_space=pl.ANY)] * len(outs)
    return pl.pallas_call(
        functools.partial(adam_kernel, rows=rows),
        out_shape=(jax.ShapeDtypeStruct(first_moment.shape, BF16),) * 3,
        grid_spec=pltpu.PrefetchScalarGridSpec(
            num_scalar_prefetch=1,
            grid=(count,),
            in_specs=[here, there, there] + held,
            out_specs=(there,) * 3,
        ),
        input_output_aliases={4 + i: i for i in range(len(outs))},
        compiler_params=pltpu.CompilerParams(vmem_limit_bytes=32 * 1024 * 1024),
        cost_estimate=pl.CostEstimate(flops=20 * gradient.size, bytes_accessed=14 * gradient.size, transcendentals=0),
    )(at, gradient, first_moment, second_moment, *outs)


def body(inputs, dec_bias, weight, enc_bias, first_moment, second_moment):
    latents, width = weight.shape
    half = width // 2
    part = half // SIDE
    x, y, c = lax.axis_index("x"), lax.axis_index("y"), lax.axis_index("c")
    zh, z = lax.axis_index("zh"), lax.axis_index(Z)
    last_me, first_me = jnp.where(c == 0, x, y), jnp.where(c == 0, y, x)
    order = jnp.array(ORDER, jnp.int32)
    behind_last = jnp.repeat((last_me - order) % SIDE, SIDE)
    behind_first = jnp.tile((first_me - order) % SIDE, SIDE)
    ahead_last = jnp.repeat((last_me + order) % SIDE, SIDE)

    def places(last):
        return jnp.stack([jnp.where(c == 0, behind_first, last), jnp.where(c == 0, last, behind_first)])

    gather_place, send_place = places(behind_last), places(ahead_last)

    kept = lax.dynamic_slice_in_dim(inputs, c * half + x * part, part, 1)
    given = swap(lax.dynamic_slice_in_dim(inputs, (1 - c) * half + x * part, part, 1))
    both = jnp.concatenate([jnp.where(c == 0, kept, given), jnp.where(c == 0, given, kept)], 0)
    count = both.shape[0]
    block = jnp.zeros((SIDE * count, part), BF16)
    block = lax.dynamic_update_slice_in_dim(block, both, zh * count, 0)
    for by in ORDER[1:]:
        arrived = lax.ppermute(both, "zh", [(i, (i + by) % SIDE) for i in range(SIDE)])
        block = lax.dynamic_update_slice_in_dim(block, arrived, (zh - by) % SIDE * count, 0)
    source = block
    thick = source.shape[0]
    rows = thick * SIDE
    pieces = spread(jnp.stack(spread(source, False)), True)

    taken = swap(lax.dynamic_slice_in_dim(weight, (1 - c) * half, half, 1))
    pair = jnp.concatenate([lax.dynamic_slice_in_dim(weight, c * half, half, 1), taken], 0)
    decoder = lax.dynamic_slice_in_dim(dec_bias, c * half, half, 0)[None, :]
    bias = jnp.concatenate([enc_bias, swap(enc_bias)])[None, :]

    centered, own = project(gather_place, pair, decoder, pieces, True)
    preact, activity, flat = call(
        activate_kernel,
        (
            jax.ShapeDtypeStruct(own.shape, F32),
            jax.ShapeDtypeStruct(own.shape, BF16),
            jax.ShapeDtypeStruct(own.shape[::-1], BF16),
        ),
        (own, swap(own), bias),
        own.size * 4,
    )

    def recon_block(slot):
        return call(
            functools.partial(recon_kernel, slot=slot),
            jax.ShapeDtypeStruct((SIDE, thick, part), BF16),
            (send_place, activity, pair),
            2 * rows * part * 2 * latents,
            [SMEM, VMEM, VMEM],
        )

    total = 0.0
    for slot in (1, 2, 3):
        total = total + shift(recon_block(slot), ORDER[slot], True).astype(F32)
    total = (total + recon_block(0).astype(F32)).astype(BF16)
    strip = total[0].astype(F32)
    for by in ORDER[1:]:
        strip = strip + shift(total[ORDER.index(SIDE - by)], by, False).astype(F32)
    thin = thick // 8
    parts = lax.all_to_all(strip.astype(BF16).reshape(8, thin, part), Z, 0, 0, tiled=True)
    recon = jnp.sum(parts.astype(F32), 0)
    here = lax.dynamic_slice_in_dim(source, z * thin, thin, 0).astype(F32)
    error = (recon + lax.dynamic_slice_in_dim(decoder, x * part, part, 1) - here).astype(BF16)
    error = lax.all_to_all(jnp.broadcast_to(error, (8, thin, part)), Z, 0, 0, tiled=True)
    pieces = spread(jnp.stack(spread(error.reshape(thick, part), False)), True)

    error, own = project(gather_place, pair, decoder, pieces, False)
    mine, theirs, _ = call(
        functools.partial(gradient_kernel, chunk=512),
        (
            jax.ShapeDtypeStruct((latents, half), F32),
            jax.ShapeDtypeStruct((latents, half), BF16),
            jax.ShapeDtypeStruct(flat.shape, BF16),
        ),
        (own, swap(own), preact, flat, error, centered),
        8 * rows * half * latents,
    )
    arrived = swap(theirs)
    at = c.astype(jnp.int32)[None]
    outs = adam(at, mine, first_moment, second_moment, (), rows)
    return tuple(adam(1 - at, arrived, first_moment, second_moment, outs, rows))


def solution(mesh):
    fine = Mesh(mesh.devices.reshape(4, 2, 4, 4, 2), ("x", "zl", "y", "zh", "c"))
    lat = ("y", "zh", "c")
    everything = ("x", "zl", "y", "zh", "c")
    return jax.shard_map(
        body,
        mesh=fine,
        in_specs=(P(lat, None), P(), P(everything, None), P(everything), P(everything, None), P(everything, None)),
        out_specs=(P(everything, None),) * 3,
        check_vma=False,
    )
```

```python
import functools

import jax
import jax.numpy as jnp
from jax import lax
from jax.experimental import pallas as pl
from jax.experimental.pallas import tpu as pltpu
from jax.sharding import Mesh, PartitionSpec as P

STEP = 100
BF16 = jnp.bfloat16
F32 = jnp.float32
SIDE = 4
CHUNKS = 2
ORDER = (0, 2, 1, 3)
PLANE = ("x", "y", "c")
Z = ("zh", "zl")
VMEM = pl.BlockSpec(memory_space=pltpu.VMEM)
SMEM = pl.BlockSpec(memory_space=pltpu.SMEM)
PARAMS = pltpu.CompilerParams(vmem_limit_bytes=48 * 1024 * 1024)


def plane_pairs(by, last):
    pairs = []
    for x in range(SIDE):
        for y in range(SIDE):
            for c in range(2):
                along_x = (c == 0) == last
                to_x = (x + by) % SIDE if along_x else x
                to_y = y if along_x else (y + by) % SIDE
                pairs.append(((x * SIDE + y) * 2 + c, (to_x * SIDE + to_y) * 2 + c))
    return pairs


def shift(value, by, last):
    return lax.ppermute(value, PLANE, plane_pairs(by, last))


def swap(value):
    return lax.ppermute(value, "c", [(0, 1), (1, 0)])


def spread(piece, last):
    return [piece] + [shift(piece, by, last) for by in ORDER[1:]]


def call(kernel, out_shape, args, flops, specs=None, params=PARAMS):
    shapes = jax.tree.leaves(out_shape)
    moved = sum(a.size * a.dtype.itemsize for a in list(args) + shapes)
    return pl.pallas_call(
        kernel,
        out_shape=out_shape,
        in_specs=specs or [VMEM] * len(args),
        out_specs=jax.tree.map(lambda _: VMEM, out_shape),
        compiler_params=params,
        cost_estimate=pl.CostEstimate(flops=flops, bytes_accessed=moved, transcendentals=0),
    )(*args)


def project_kernel(place, weight, extra, *refs, centre):
    pieces, (laid, product) = refs[:SIDE], refs[SIDE:]
    thick, part = pieces[0].shape[1:]
    for i, piece in enumerate(pieces):

        def step(j, carry, i=i, piece=piece):
            row = pl.multiple_of(place[0, i * SIDE + j] * thick, thick)
            column = pl.multiple_of(place[1, i * SIDE + j] * part, part)
            block = piece[j]
            if centre:
                block = (block.astype(F32) - extra[:, pl.ds(column, part)]).astype(BF16)
            laid[pl.ds(row, thick), pl.ds(column, part)] = block
            return carry

        lax.fori_loop(0, SIDE, step, 0)
    total = None
    for q in range(SIDE):
        columns = pl.ds(q * part, part)
        term = lax.dot_general(
            laid[:, columns], weight[:, columns], (((1,), (1,)), ((), ())), preferred_element_type=F32
        )
        total = term if total is None else total + term
    product[...] = total


def project(place, weight, extra, pieces, centre):
    thick, part = pieces[0].shape[1:]
    rows, width = thick * SIDE, part * SIDE
    return call(
        functools.partial(project_kernel, centre=centre),
        (jax.ShapeDtypeStruct((rows, width), BF16), jax.ShapeDtypeStruct((rows, weight.shape[0]), F32)),
        (place, weight, extra, *pieces),
        2 * rows * width * weight.shape[0],
        [SMEM] + [VMEM] * (2 + SIDE),
    )


def join(own, other, latents):
    return jnp.concatenate([own[:, :latents] + other[:, latents:], own[:, latents:] + other[:, :latents]], 1)


def recon_kernel(place, own, other, bias, weight, preact, flat, *refs):
    blocks, (activity, laid) = refs[:SIDE], refs[SIDE:]
    _, thick, part = blocks[0].shape
    value = join(own[...], other[...], bias.shape[1] // 2) + bias[...]
    preact[...] = value
    positive = jnp.maximum(value, 0.0)
    activity[...] = positive.astype(BF16)
    flat[...] = positive.T.astype(BF16)
    for q in range(SIDE):
        columns = pl.ds(q * part, part)
        laid[:, columns] = jnp.dot(activity[...], weight[:, columns], preferred_element_type=F32).astype(BF16)
    for i, block in enumerate(blocks):

        def step(j, carry, i=i, block=block):
            row = pl.multiple_of(place[0, i * SIDE + j] * thick, thick)
            column = pl.multiple_of(place[1, i * SIDE + j] * part, part)
            block[j] = laid[pl.ds(row, thick), pl.ds(column, part)]
            return carry

        lax.fori_loop(0, SIDE, step, 0)


def recon(place, own, other, bias, weight):
    rows, wide = own.shape
    width = weight.shape[1]
    blocks = jax.ShapeDtypeStruct((SIDE, rows // SIDE, width // SIDE), BF16)
    args = (place, own, other, bias, weight)
    shapes = (jax.ShapeDtypeStruct((rows, wide), F32), jax.ShapeDtypeStruct((wide, rows), BF16)) + (blocks,) * SIDE
    return pl.pallas_call(
        recon_kernel,
        out_shape=shapes,
        in_specs=[SMEM] + [VMEM] * 4,
        out_specs=(VMEM,) * len(shapes),
        scratch_shapes=[pltpu.VMEM((rows, wide), BF16), pltpu.VMEM((rows, width), BF16)],
        compiler_params=PARAMS,
        cost_estimate=pl.CostEstimate(flops=2 * rows * wide * width, bytes_accessed=4 * rows * width, transcendentals=0),
    )(*args)


def gradient_kernel(own, other, preact, flat, error, centered, *refs, chunk, final):
    slope = refs[-1]
    latents = preact.shape[1] // 2
    value = jnp.where(preact[...] > 0, join(own[...], other[...], latents), 0.0)
    slope[...] = value.T.astype(BF16)

    def step(j, carry):
        columns = pl.ds(pl.multiple_of(j * chunk, chunk), chunk)
        total = jnp.dot(flat[...], error[:, columns], preferred_element_type=F32)
        total += jnp.dot(slope[...], centered[:, columns], preferred_element_type=F32)
        if final:
            before, mine, theirs = refs[:3]
            total += before[:, columns]
            mine[:, columns] = total[:latents]
            theirs[:, columns] = total[latents:].astype(BF16)
        else:
            refs[0][:, columns] = total
        return carry

    lax.fori_loop(0, error.shape[1] // chunk, step, 0)


def gradient(args, before, chunk=1024):
    flat, error = args[3], args[4]
    wide, width = flat.shape[0], error.shape[1]
    if before is None:
        shapes = jax.ShapeDtypeStruct((wide, width), F32)
    else:
        args = args + (before,)
        shapes = (jax.ShapeDtypeStruct((wide // 2, width), F32), jax.ShapeDtypeStruct((wide // 2, width), BF16))
    return pl.pallas_call(
        functools.partial(gradient_kernel, chunk=chunk, final=before is not None),
        out_shape=shapes,
        in_specs=[VMEM] * len(args),
        out_specs=jax.tree.map(lambda _: VMEM, shapes),
        scratch_shapes=[pltpu.VMEM(flat.shape, BF16)],
        compiler_params=PARAMS,
        cost_estimate=pl.CostEstimate(flops=4 * flat.size * width, bytes_accessed=12 * error.size, transcendentals=0),
    )(*args)


def adam_kernel(at, gradient_ref, first_ref, second_ref, *refs, rows):
    update_out, first_out, second_out = refs[-3:]
    gradient = gradient_ref[...].astype(F32) * (1.0 / rows)
    first = 0.9 * first_ref[...].astype(F32) + 0.1 * gradient
    second = 0.999 * second_ref[...].astype(F32) + 0.001 * gradient * gradient
    update = first * (1.0 / (1.0 - 0.9**STEP)) / (jnp.sqrt(second * (1.0 / (1.0 - 0.999**STEP))) + 1e-08)
    update_out[...] = update.astype(BF16)
    first_out[...] = first.astype(BF16)
    second_out[...] = second.astype(BF16)


def adam(at, gradient, first_moment, second_moment, outs, rows, chunk=512):
    latents, width = gradient.shape
    count = width // chunk
    here = pl.BlockSpec((latents, chunk), lambda i, at: (0, i))
    there = pl.BlockSpec((latents, chunk), lambda i, at: (0, at[0] * count + i))
    held = [pl.BlockSpec(memory_space=pl.ANY)] * len(outs)
    return pl.pallas_call(
        functools.partial(adam_kernel, rows=rows),
        out_shape=(jax.ShapeDtypeStruct(first_moment.shape, BF16),) * 3,
        grid_spec=pltpu.PrefetchScalarGridSpec(
            num_scalar_prefetch=1,
            grid=(count,),
            in_specs=[here, there, there] + held,
            out_specs=(there,) * 3,
        ),
        input_output_aliases={4 + i: i for i in range(len(outs))},
        compiler_params=pltpu.CompilerParams(vmem_limit_bytes=32 * 1024 * 1024),
        cost_estimate=pl.CostEstimate(flops=20 * gradient.size, bytes_accessed=14 * gradient.size, transcendentals=0),
    )(at, gradient, first_moment, second_moment, *outs)


def body(inputs, dec_bias, weight, enc_bias, first_moment, second_moment):
    latents, width = weight.shape
    half = width // 2
    part = half // SIDE
    x, y, c = lax.axis_index("x"), lax.axis_index("y"), lax.axis_index("c")
    zh, z = lax.axis_index("zh"), lax.axis_index(Z)
    last_me, first_me = jnp.where(c == 0, x, y), jnp.where(c == 0, y, x)
    order = jnp.array(ORDER, jnp.int32)
    behind_last = jnp.repeat((last_me - order) % SIDE, SIDE)
    behind_first = jnp.tile((first_me - order) % SIDE, SIDE)
    ahead_last = jnp.repeat((last_me + order) % SIDE, SIDE)

    def places(last):
        return jnp.stack([jnp.where(c == 0, behind_first, last), jnp.where(c == 0, last, behind_first)])

    gather_place, send_place = places(behind_last), places(ahead_last)

    kept = lax.dynamic_slice_in_dim(inputs, c * half + x * part, part, 1)
    given = swap(lax.dynamic_slice_in_dim(inputs, (1 - c) * half + x * part, part, 1))
    both = jnp.concatenate([jnp.where(c == 0, kept, given), jnp.where(c == 0, given, kept)], 0)
    count = both.shape[0]
    block = jnp.zeros((SIDE * count, part), BF16)
    block = lax.dynamic_update_slice_in_dim(block, both, zh * count, 0)
    for by in ORDER[1:]:
        arrived = lax.ppermute(both, "zh", [(i, (i + by) % SIDE) for i in range(SIDE)])
        block = lax.dynamic_update_slice_in_dim(block, arrived, (zh - by) % SIDE * count, 0)
    source = block
    split = source.shape[0] // CHUNKS
    gathered = spread(source, False)

    taken = swap(lax.dynamic_slice_in_dim(weight, (1 - c) * half, half, 1))
    pair = jnp.concatenate([lax.dynamic_slice_in_dim(weight, c * half, half, 1), taken], 0)
    decoder = lax.dynamic_slice_in_dim(dec_bias, c * half, half, 0)[None, :]
    bias = jnp.concatenate([enc_bias, swap(enc_bias)])[None, :]
    rows = source.shape[0] * SIDE
    thin = split // 8
    share = lax.dynamic_slice_in_dim(decoder, x * part, part, 1)

    def reduce(blocks):
        total = blocks[0].astype(F32)
        for slot in (1, 2, 3):
            total = total + shift(blocks[slot], ORDER[slot], True).astype(F32)
        total = total.astype(BF16)
        strip = total[0].astype(F32)
        for by in ORDER[1:]:
            strip = strip + shift(total[ORDER.index(SIDE - by)], by, False).astype(F32)
        return lax.all_to_all(strip.astype(BF16).reshape(8, thin, part), Z, 0, 0, tiled=True)

    def expand(parts, k):
        recon_sum = jnp.sum(parts.astype(F32), 0)
        here = lax.dynamic_slice_in_dim(source, k * split + z * thin, thin, 0).astype(F32)
        error = (recon_sum + share - here).astype(BF16)
        error = lax.all_to_all(jnp.broadcast_to(error, (8, thin, part)), Z, 0, 0, tiled=True)
        return spread(jnp.stack(spread(error.reshape(split, part), False)), True)

    chunks = range(CHUNKS)
    pieces = [spread(jnp.stack([g[k * split : (k + 1) * split] for g in gathered]), True) for k in chunks]
    first = [project(gather_place, pair, decoder, pieces[k], True) for k in chunks]
    made = [recon(send_place, first[k][1], swap(first[k][1]), bias, pair) for k in chunks]
    parts = [reduce(made[k][2:]) for k in chunks]
    pieces = [expand(parts[k], k) for k in chunks]
    second = [project(gather_place, pair, decoder, pieces[k], False) for k in chunks]
    total = None
    for k in chunks:
        error, own = second[k]
        total = gradient((own, swap(own), made[k][0], made[k][1], error, first[k][0]), total)
    mine, theirs = total
    arrived = swap(theirs)
    at = c.astype(jnp.int32)[None]
    outs = adam(at, mine, first_moment, second_moment, (), rows)
    return tuple(adam(1 - at, arrived, first_moment, second_moment, outs, rows))


def solution(mesh):
    fine = Mesh(mesh.devices.reshape(4, 2, 4, 4, 2), ("x", "zl", "y", "zh", "c"))
    lat = ("y", "zh", "c")
    everything = ("x", "zl", "y", "zh", "c")
    return jax.shard_map(
        body,
        mesh=fine,
        in_specs=(P(lat, None), P(), P(everything, None), P(everything), P(everything, None), P(everything, None)),
        out_specs=(P(everything, None),) * 3,
        check_vma=False,
    )
```

```python
import functools

import jax
import jax.numpy as jnp
from jax import lax
from jax.experimental import pallas as pl
from jax.experimental.pallas import tpu as pltpu
from jax.sharding import Mesh, PartitionSpec as P

STEP = 100
BF16 = jnp.bfloat16
F32 = jnp.float32
SIDE = 4
CHUNKS = 2
ORDER = (0, 2, 1, 3)
PLANE = ("x", "y", "c")
Z = ("zh", "zl")
VMEM = pl.BlockSpec(memory_space=pltpu.VMEM)
SMEM = pl.BlockSpec(memory_space=pltpu.SMEM)
PARAMS = pltpu.CompilerParams(vmem_limit_bytes=16 * 1024 * 1024)


def plane_pairs(by, last):
    pairs = []
    for x in range(SIDE):
        for y in range(SIDE):
            for c in range(2):
                along_x = (c == 0) == last
                to_x = (x + by) % SIDE if along_x else x
                to_y = y if along_x else (y + by) % SIDE
                pairs.append(((x * SIDE + y) * 2 + c, (to_x * SIDE + to_y) * 2 + c))
    return pairs


def shift(value, by, last):
    return lax.ppermute(value, PLANE, plane_pairs(by, last))


def swap(value):
    return lax.ppermute(value, "c", [(0, 1), (1, 0)])


def spread(piece, last):
    return [piece] + [shift(piece, by, last) for by in ORDER[1:]]


def project_kernel(place, weight, extra, lift, *refs, centre):
    pieces, (laid, product) = refs[:SIDE], refs[-2:]
    thick, part = pieces[0].shape[1:]
    for i, piece in enumerate(pieces):

        def step(j, carry, i=i, piece=piece):
            row = pl.multiple_of(place[0, i * SIDE + j] * thick, thick)
            column = pl.multiple_of(place[1, i * SIDE + j] * part, part)
            block = piece[j]
            if centre:
                block = (block.astype(F32) - extra[:, pl.ds(column, part)]).astype(BF16)
            laid[pl.ds(row, thick), pl.ds(column, part)] = block
            return carry

        lax.fori_loop(0, SIDE, step, 0)
    total = lift[...] if centre else None
    for q in range(SIDE):
        columns = pl.ds(q * part, part)
        term = lax.dot_general(
            laid[:, columns], weight[:, columns], (((1,), (1,)), ((), ())), preferred_element_type=F32
        )
        total = term if total is None else total + term
    product[...] = total


def project(place, weight, extra, lift, pieces, centre, after=()):
    thick, part = pieces[0].shape[1:]
    rows, width = thick * SIDE, part * SIDE
    args = (place, weight, extra, lift, *pieces, *after)
    return pl.pallas_call(
        functools.partial(project_kernel, centre=centre),
        out_shape=(jax.ShapeDtypeStruct((rows, width), BF16), jax.ShapeDtypeStruct((rows, weight.shape[0]), F32)),
        in_specs=[SMEM] + [VMEM] * (3 + SIDE) + [pl.BlockSpec(memory_space=pl.ANY)] * len(after),
        out_specs=(VMEM, VMEM),
        compiler_params=PARAMS,
        cost_estimate=pl.CostEstimate(
            flops=2 * rows * width * weight.shape[0], bytes_accessed=4 * rows * width, transcendentals=0
        ),
    )(*args)


def join(own, other, latents):
    return jnp.concatenate([own[:, :latents] + other[:, latents:], own[:, latents:] + other[:, :latents]], 1)


def recon_kernel(place, own, other, weight, preact, flat, *refs):
    blocks, (activity, laid) = refs[:SIDE], refs[SIDE:]
    _, thick, part = blocks[0].shape
    value = join(own[...], other[...], own.shape[1] // 2)
    preact[...] = value
    positive = jnp.maximum(value, 0.0)
    activity[...] = positive.astype(BF16)
    flat[...] = positive.T.astype(BF16)
    for q in range(SIDE):
        columns = pl.ds(q * part, part)
        laid[:, columns] = jnp.dot(activity[...], weight[:, columns], preferred_element_type=F32).astype(BF16)
    for i, block in enumerate(blocks):

        def step(j, carry, i=i, block=block):
            row = pl.multiple_of(place[0, i * SIDE + j] * thick, thick)
            column = pl.multiple_of(place[1, i * SIDE + j] * part, part)
            block[j] = laid[pl.ds(row, thick), pl.ds(column, part)]
            return carry

        lax.fori_loop(0, SIDE, step, 0)


def recon(place, own, other, weight):
    rows, wide = own.shape
    width = weight.shape[1]
    blocks = jax.ShapeDtypeStruct((SIDE, rows // SIDE, width // SIDE), BF16)
    args = (place, own, other, weight)
    shapes = (jax.ShapeDtypeStruct((rows, wide), F32), jax.ShapeDtypeStruct((wide, rows), BF16)) + (blocks,) * SIDE
    return pl.pallas_call(
        recon_kernel,
        out_shape=shapes,
        in_specs=[SMEM] + [VMEM] * 3,
        out_specs=(VMEM,) * len(shapes),
        scratch_shapes=[pltpu.VMEM((rows, wide), BF16), pltpu.VMEM((rows, width), BF16)],
        compiler_params=PARAMS,
        cost_estimate=pl.CostEstimate(flops=2 * rows * wide * width, bytes_accessed=4 * rows * width, transcendentals=0),
    )(*args)


def gradient_kernel(own, other, preact, flat, error, centered, *refs, chunk, final):
    slope = refs[-1]
    latents = preact.shape[1] // 2
    value = jnp.where(preact[...] > 0, join(own[...], other[...], latents), 0.0)
    slope[...] = value.T.astype(BF16)

    def step(j, carry):
        columns = pl.ds(pl.multiple_of(j * chunk, chunk), chunk)
        total = jnp.dot(flat[...], error[:, columns], preferred_element_type=F32)
        total += jnp.dot(slope[...], centered[:, columns], preferred_element_type=F32)
        if final:
            before, mine, theirs = refs[:3]
            total += before[:, columns]
            mine[:, columns] = total[:latents]
            theirs[:, columns] = total[latents:].astype(BF16)
        else:
            refs[0][:, columns] = total
        return carry

    lax.fori_loop(0, error.shape[1] // chunk, step, 0)


def gradient(args, before, chunk=1024):
    flat, error = args[3], args[4]
    wide, width = flat.shape[0], error.shape[1]
    if before is None:
        shapes = jax.ShapeDtypeStruct((wide, width), F32)
    else:
        args = args + (before,)
        shapes = (jax.ShapeDtypeStruct((wide // 2, width), F32), jax.ShapeDtypeStruct((wide // 2, width), BF16))
    return pl.pallas_call(
        functools.partial(gradient_kernel, chunk=chunk, final=before is not None),
        out_shape=shapes,
        in_specs=[VMEM] * len(args),
        out_specs=jax.tree.map(lambda _: VMEM, shapes),
        scratch_shapes=[pltpu.VMEM(flat.shape, BF16)],
        compiler_params=PARAMS,
        cost_estimate=pl.CostEstimate(flops=4 * flat.size * width, bytes_accessed=12 * error.size, transcendentals=0),
    )(*args)


def adam_kernel(at, gradient_ref, first_ref, second_ref, *refs, rows):
    update_out, first_out, second_out = refs[-3:]
    gradient = gradient_ref[...].astype(F32) * (1.0 / rows)
    first = 0.9 * first_ref[...].astype(F32) + 0.1 * gradient
    second = 0.999 * second_ref[...].astype(F32) + 0.001 * gradient * gradient
    update = first * (1.0 / (1.0 - 0.9**STEP)) / (jnp.sqrt(second * (1.0 / (1.0 - 0.999**STEP))) + 1e-08)
    update_out[...] = update.astype(BF16)
    first_out[...] = first.astype(BF16)
    second_out[...] = second.astype(BF16)


def adam(at, gradient, first_moment, second_moment, outs, rows, chunk=1024):
    latents, width = gradient.shape
    count = width // chunk
    here = pl.BlockSpec((latents, chunk), lambda i, at: (0, i))
    there = pl.BlockSpec((latents, chunk), lambda i, at: (0, at[0] * count + i))
    held = [pl.BlockSpec(memory_space=pl.ANY)] * len(outs)
    return pl.pallas_call(
        functools.partial(adam_kernel, rows=rows),
        out_shape=(jax.ShapeDtypeStruct(first_moment.shape, BF16),) * 3,
        grid_spec=pltpu.PrefetchScalarGridSpec(
            num_scalar_prefetch=1,
            grid=(count,),
            in_specs=[here, there, there] + held,
            out_specs=(there,) * 3,
        ),
        input_output_aliases={4 + i: i for i in range(len(outs))},
        compiler_params=pltpu.CompilerParams(vmem_limit_bytes=32 * 1024 * 1024),
        cost_estimate=pl.CostEstimate(flops=20 * gradient.size, bytes_accessed=14 * gradient.size, transcendentals=0),
    )(at, gradient, first_moment, second_moment, *outs)


def body(inputs, dec_bias, weight, enc_bias, first_moment, second_moment):
    latents, width = weight.shape
    half = width // 2
    part = half // SIDE
    x, y, c = lax.axis_index("x"), lax.axis_index("y"), lax.axis_index("c")
    z = lax.axis_index(Z)
    last_me, first_me = jnp.where(c == 0, x, y), jnp.where(c == 0, y, x)
    order = jnp.array(ORDER, jnp.int32)
    behind_last = jnp.repeat((last_me - order) % SIDE, SIDE)
    behind_first = jnp.tile((first_me - order) % SIDE, SIDE)
    ahead_last = jnp.repeat((last_me + order) % SIDE, SIDE)

    def places(last):
        return jnp.stack([jnp.where(c == 0, behind_first, last), jnp.where(c == 0, last, behind_first)])

    gather_place, send_place = places(behind_last), places(ahead_last)

    own_columns = [lax.dynamic_slice_in_dim(inputs, core * half + x * part, part, 1) for core in range(2)]
    block = jnp.broadcast_to(jnp.stack(own_columns), (SIDE, 2) + own_columns[0].shape)
    block = lax.all_to_all(block.reshape((8,) + own_columns[0].shape), ("zh", "c"), 0, 0, tiled=True)
    block = block.reshape(-1, part)
    source = block
    split = source.shape[0] // CHUNKS
    gathered = spread(source, False)

    taken = swap(lax.dynamic_slice_in_dim(weight, (1 - c) * half, half, 1))
    pair = jnp.concatenate([lax.dynamic_slice_in_dim(weight, c * half, half, 1), taken], 0)
    decoder = lax.dynamic_slice_in_dim(dec_bias, c * half, half, 0)[None, :]
    lift = jnp.concatenate([enc_bias, jnp.zeros_like(enc_bias)])[None, :]
    rows = source.shape[0] * SIDE
    thin = split // 8
    share = lax.dynamic_slice_in_dim(decoder, x * part, part, 1)

    def reduce(blocks):
        total = blocks[0].astype(F32)
        for slot in (1, 2, 3):
            total = total + shift(blocks[slot], ORDER[slot], True).astype(F32)
        total = total.astype(BF16)
        strip = total[0].astype(F32)
        for by in ORDER[1:]:
            strip = strip + shift(total[ORDER.index(SIDE - by)], by, False).astype(F32)
        return strip.astype(BF16).reshape(8, thin, part)

    chunks = range(CHUNKS)
    pieces = [spread(jnp.stack([g[k * split : (k + 1) * split] for g in gathered]), True) for k in chunks]
    ahead = [project(gather_place, pair, decoder, lift, pieces[k], True) for k in chunks]
    made = [recon(send_place, ahead[k][1], swap(ahead[k][1]), pair) for k in chunks]
    parts = jnp.concatenate([reduce(made[k][2:]) for k in chunks], 1)
    recon_sum = jnp.sum(lax.all_to_all(parts, Z, 0, 0, tiled=True).astype(F32), 0)
    here = [lax.dynamic_slice_in_dim(source, k * split + z * thin, thin, 0) for k in chunks]
    error = (recon_sum + share - jnp.concatenate(here, 0).astype(F32)).astype(BF16)
    error = lax.all_to_all(jnp.broadcast_to(error, (8,) + error.shape), Z, 0, 0, tiled=True)
    error = [error[:, k * thin : (k + 1) * thin].reshape(split, part) for k in chunks]
    pieces = [spread(jnp.stack(spread(error[k], False)), True) for k in chunks]
    total = None
    for k in chunks:
        after = () if total is None else (total,)
        laid, own = project(gather_place, pair, decoder, lift, pieces[k], False, after)
        total = gradient((own, swap(own), made[k][0], made[k][1], laid, ahead[k][0]), total)
    mine, theirs = total
    arrived = swap(theirs)
    at = c.astype(jnp.int32)[None]
    outs = adam(at, mine, first_moment, second_moment, (), rows)
    return tuple(adam(1 - at, arrived, first_moment, second_moment, outs, rows))


def solution(mesh):
    fine = Mesh(mesh.devices.reshape(4, 2, 4, 4, 2), ("x", "zl", "y", "zh", "c"))
    lat = ("y", "zh", "c")
    everything = ("x", "zl", "y", "zh", "c")
    return jax.shard_map(
        body,
        mesh=fine,
        in_specs=(P(lat, None), P(), P(everything, None), P(everything), P(everything, None), P(everything, None)),
        out_specs=(P(everything, None),) * 3,
        check_vma=False,
    )
```

```python
import functools

import jax
import jax.numpy as jnp
from jax import lax
from jax.experimental import pallas as pl
from jax.experimental.pallas import tpu as pltpu
from jax.sharding import Mesh, PartitionSpec as P

STEP = 100
BF16 = jnp.bfloat16
F32 = jnp.float32
SIDE = 4
CHUNKS = 2
ORDER = (0, 2, 1, 3)
PLANE = ("x", "y", "c")
Z = ("zh", "zl")
VMEM = pl.BlockSpec(memory_space=pltpu.VMEM)
SMEM = pl.BlockSpec(memory_space=pltpu.SMEM)
PARAMS = pltpu.CompilerParams(vmem_limit_bytes=8 * 1024 * 1024)


def plane_pairs(by, last):
    pairs = []
    for x in range(SIDE):
        for y in range(SIDE):
            for c in range(2):
                along_x = (c == 0) == last
                to_x = (x + by) % SIDE if along_x else x
                to_y = y if along_x else (y + by) % SIDE
                pairs.append(((x * SIDE + y) * 2 + c, (to_x * SIDE + to_y) * 2 + c))
    return pairs


def shift(value, by, last):
    return lax.ppermute(value, PLANE, plane_pairs(by, last))


def swap(value):
    return lax.ppermute(value, "c", [(0, 1), (1, 0)])


def spread(piece, last):
    return [piece] + [shift(piece, by, last) for by in ORDER[1:]]


def project_kernel(place, weight, extra, lift, *refs, centre):
    pieces, (laid, product) = refs[:SIDE], refs[-2:]
    thick, part = pieces[0].shape[1:]
    for i, piece in enumerate(pieces):

        def step(j, carry, i=i, piece=piece):
            row = pl.multiple_of(place[0, i * SIDE + j] * thick, thick)
            column = pl.multiple_of(place[1, i * SIDE + j] * part, part)
            block = piece[j]
            if centre:
                block = (block.astype(F32) - extra[:, pl.ds(column, part)]).astype(BF16)
            laid[pl.ds(row, thick), pl.ds(column, part)] = block
            return carry

        lax.fori_loop(0, SIDE, step, 0)
    total = lift[...] if centre else None
    for q in range(SIDE):
        columns = pl.ds(q * part, part)
        term = lax.dot_general(
            laid[:, columns], weight[:, columns], (((1,), (1,)), ((), ())), preferred_element_type=F32
        )
        total = term if total is None else total + term
    product[...] = total


def project(place, weight, extra, lift, pieces, centre, after=()):
    thick, part = pieces[0].shape[1:]
    rows, width = thick * SIDE, part * SIDE
    args = (place, weight, extra, lift, *pieces, *after)
    return pl.pallas_call(
        functools.partial(project_kernel, centre=centre),
        out_shape=(jax.ShapeDtypeStruct((rows, width), BF16), jax.ShapeDtypeStruct((rows, weight.shape[0]), F32)),
        in_specs=[SMEM] + [VMEM] * (3 + SIDE) + [pl.BlockSpec(memory_space=pl.ANY)] * len(after),
        out_specs=(VMEM, VMEM),
        compiler_params=PARAMS,
        cost_estimate=pl.CostEstimate(
            flops=2 * rows * width * weight.shape[0], bytes_accessed=4 * rows * width, transcendentals=0
        ),
    )(*args)


def join(own, other, latents):
    return jnp.concatenate([own[:, :latents] + other[:, latents:], own[:, latents:] + other[:, :latents]], 1)


def recon_kernel(place, own, other, weight, preact, flat, *refs):
    blocks, (activity, laid) = refs[:SIDE], refs[SIDE:]
    _, thick, part = blocks[0].shape
    value = join(own[...], other[...], own.shape[1] // 2)
    preact[...] = value
    positive = jnp.maximum(value, 0.0)
    activity[...] = positive.astype(BF16)
    flat[...] = positive.T.astype(BF16)
    for q in range(SIDE):
        columns = pl.ds(q * part, part)
        laid[:, columns] = jnp.dot(activity[...], weight[:, columns], preferred_element_type=F32).astype(BF16)
    for i, block in enumerate(blocks):

        def step(j, carry, i=i, block=block):
            row = pl.multiple_of(place[0, i * SIDE + j] * thick, thick)
            column = pl.multiple_of(place[1, i * SIDE + j] * part, part)
            block[j] = laid[pl.ds(row, thick), pl.ds(column, part)]
            return carry

        lax.fori_loop(0, SIDE, step, 0)


def recon(place, own, other, weight):
    rows, wide = own.shape
    width = weight.shape[1]
    blocks = jax.ShapeDtypeStruct((SIDE, rows // SIDE, width // SIDE), BF16)
    args = (place, own, other, weight)
    shapes = (jax.ShapeDtypeStruct((rows, wide), F32), jax.ShapeDtypeStruct((wide, rows), BF16)) + (blocks,) * SIDE
    return pl.pallas_call(
        recon_kernel,
        out_shape=shapes,
        in_specs=[SMEM] + [VMEM] * 3,
        out_specs=(VMEM,) * len(shapes),
        scratch_shapes=[pltpu.VMEM((rows, wide), BF16), pltpu.VMEM((rows, width), BF16)],
        compiler_params=PARAMS,
        cost_estimate=pl.CostEstimate(flops=2 * rows * wide * width, bytes_accessed=4 * rows * width, transcendentals=0),
    )(*args)


def gradient_kernel(own, other, preact, flat, error, centered, *refs, chunk, final):
    slope = refs[-1]
    latents = preact.shape[1] // 2
    value = jnp.where(preact[...] > 0, join(own[...], other[...], latents), 0.0)
    slope[...] = value.T.astype(BF16)

    def step(j, carry):
        columns = pl.ds(pl.multiple_of(j * chunk, chunk), chunk)
        total = jnp.dot(flat[...], error[:, columns], preferred_element_type=F32)
        total += jnp.dot(slope[...], centered[:, columns], preferred_element_type=F32)
        if final:
            before, mine, theirs = refs[:3]
            total += before[:, columns]
            mine[:, columns] = total[:latents]
            theirs[:, columns] = total[latents:].astype(BF16)
        else:
            refs[0][:, columns] = total
        return carry

    lax.fori_loop(0, error.shape[1] // chunk, step, 0)


def gradient(args, before, chunk=1024):
    flat, error = args[3], args[4]
    wide, width = flat.shape[0], error.shape[1]
    if before is None:
        shapes = jax.ShapeDtypeStruct((wide, width), F32)
    else:
        args = args + (before,)
        shapes = (jax.ShapeDtypeStruct((wide // 2, width), F32), jax.ShapeDtypeStruct((wide // 2, width), BF16))
    return pl.pallas_call(
        functools.partial(gradient_kernel, chunk=chunk, final=before is not None),
        out_shape=shapes,
        in_specs=[VMEM] * len(args),
        out_specs=jax.tree.map(lambda _: VMEM, shapes),
        scratch_shapes=[pltpu.VMEM(flat.shape, BF16)],
        compiler_params=PARAMS,
        cost_estimate=pl.CostEstimate(flops=4 * flat.size * width, bytes_accessed=12 * error.size, transcendentals=0),
    )(*args)


def adam_kernel(at, gradient_ref, first_ref, second_ref, *refs, rows):
    update_out, first_out, second_out = refs[-3:]
    gradient = gradient_ref[...].astype(F32) * (1.0 / rows)
    first = 0.9 * first_ref[...].astype(F32) + 0.1 * gradient
    second = 0.999 * second_ref[...].astype(F32) + 0.001 * gradient * gradient
    update = first * (1.0 / (1.0 - 0.9**STEP)) / (jnp.sqrt(second * (1.0 / (1.0 - 0.999**STEP))) + 1e-08)
    update_out[...] = update.astype(BF16)
    first_out[...] = first.astype(BF16)
    second_out[...] = second.astype(BF16)


def adam(at, gradient, first_moment, second_moment, outs, rows, chunk=1024):
    latents, width = gradient.shape
    count = width // chunk
    here = pl.BlockSpec((latents, chunk), lambda i, at: (0, i))
    there = pl.BlockSpec((latents, chunk), lambda i, at: (0, at[0] * count + i))
    held = [pl.BlockSpec(memory_space=pl.ANY)] * len(outs)
    return pl.pallas_call(
        functools.partial(adam_kernel, rows=rows),
        out_shape=(jax.ShapeDtypeStruct(first_moment.shape, BF16),) * 3,
        grid_spec=pltpu.PrefetchScalarGridSpec(
            num_scalar_prefetch=1,
            grid=(count,),
            in_specs=[here, there, there] + held,
            out_specs=(there,) * 3,
        ),
        input_output_aliases={4 + i: i for i in range(len(outs))},
        compiler_params=PARAMS,
        cost_estimate=pl.CostEstimate(flops=20 * gradient.size, bytes_accessed=14 * gradient.size, transcendentals=0),
    )(at, gradient, first_moment, second_moment, *outs)


def body(inputs, dec_bias, weight, enc_bias, first_moment, second_moment):
    latents, width = weight.shape
    half = width // 2
    part = half // SIDE
    x, y, c = lax.axis_index("x"), lax.axis_index("y"), lax.axis_index("c")
    z = lax.axis_index(Z)
    last_me, first_me = jnp.where(c == 0, x, y), jnp.where(c == 0, y, x)
    order = jnp.array(ORDER, jnp.int32)
    behind_last = jnp.repeat((last_me - order) % SIDE, SIDE)
    behind_first = jnp.tile((first_me - order) % SIDE, SIDE)
    ahead_last = jnp.repeat((last_me + order) % SIDE, SIDE)

    def places(last):
        return jnp.stack([jnp.where(c == 0, behind_first, last), jnp.where(c == 0, last, behind_first)])

    gather_place, send_place = places(behind_last), places(ahead_last)

    own_columns = [lax.dynamic_slice_in_dim(inputs, core * half + x * part, part, 1) for core in range(2)]
    block = jnp.broadcast_to(jnp.stack(own_columns), (SIDE, 2) + own_columns[0].shape)
    block = lax.all_to_all(block.reshape((8,) + own_columns[0].shape), ("zh", "c"), 0, 0, tiled=True)
    block = block.reshape(-1, part)
    source = block
    split = source.shape[0] // CHUNKS
    gathered = spread(source, False)

    taken = swap(lax.dynamic_slice_in_dim(weight, (1 - c) * half, half, 1))
    pair = jnp.concatenate([lax.dynamic_slice_in_dim(weight, c * half, half, 1), taken], 0)
    decoder = lax.dynamic_slice_in_dim(dec_bias, c * half, half, 0)[None, :]
    lift = jnp.concatenate([enc_bias, jnp.zeros_like(enc_bias)])[None, :]
    rows = source.shape[0] * SIDE
    thin = split // 8
    share = lax.dynamic_slice_in_dim(decoder, x * part, part, 1)

    def reduce(blocks):
        total = blocks[0].astype(F32)
        for slot in (1, 2, 3):
            total = total + shift(blocks[slot], ORDER[slot], True).astype(F32)
        return total.astype(BF16)

    def fan(gathered):
        return [spread(jnp.stack([g[k * split : (k + 1) * split] for g in gathered]), True) for k in chunks]

    chunks = range(CHUNKS)
    pieces = fan(gathered)
    ahead = [project(gather_place, pair, decoder, lift, pieces[k], True) for k in chunks]
    made = [recon(send_place, ahead[k][1], swap(ahead[k][1]), pair) for k in chunks]
    blocks = jnp.concatenate([reduce(made[k][2:]) for k in chunks], 1)
    strip = blocks[0].astype(F32)
    for by in ORDER[1:]:
        strip = strip + shift(blocks[ORDER.index(SIDE - by)], by, False).astype(F32)
    parts = lax.all_to_all(strip.astype(BF16).reshape(8, CHUNKS * thin, part), Z, 0, 0, tiled=True)
    recon_sum = jnp.sum(parts.astype(F32), 0)
    here = lax.dynamic_slice_in_dim(source, z * CHUNKS * thin, CHUNKS * thin, 0).astype(F32)
    error = (recon_sum + share - here).astype(BF16)
    error = lax.all_to_all(jnp.broadcast_to(error, (8,) + error.shape), Z, 0, 0, tiled=True)
    pieces = fan(spread(error.reshape(-1, part), False))
    total = None
    for k in chunks:
        after = () if total is None else (total,)
        laid, own = project(gather_place, pair, decoder, lift, pieces[k], False, after)
        total = gradient((own, swap(own), made[k][0], made[k][1], laid, ahead[k][0]), total)
    mine, theirs = total
    arrived = swap(theirs)
    at = c.astype(jnp.int32)[None]
    outs = adam(at, mine, first_moment, second_moment, (), rows)
    return tuple(adam(1 - at, arrived, first_moment, second_moment, outs, rows))


def solution(mesh):
    fine = Mesh(mesh.devices.reshape(4, 2, 4, 4, 2), ("x", "zl", "y", "zh", "c"))
    lat = ("y", "zh", "c")
    everything = ("x", "zl", "y", "zh", "c")
    return jax.shard_map(
        body,
        mesh=fine,
        in_specs=(P(lat, None), P(), P(everything, None), P(everything), P(everything, None), P(everything, None)),
        out_specs=(P(everything, None),) * 3,
        check_vma=False,
    )
```

```python
import functools

import jax
import jax.numpy as jnp
from jax import lax
from jax.experimental import pallas as pl
from jax.experimental.pallas import tpu as pltpu
from jax.sharding import Mesh, PartitionSpec as P

STEP = 100
BF16 = jnp.bfloat16
F32 = jnp.float32
SIDE = 4
CHUNKS = 2
ORDER = (0, 2, 1, 3)
PLANE = ("x", "y", "c")
Z = ("zh", "zl")
VMEM = pl.BlockSpec(memory_space=pltpu.VMEM)
SMEM = pl.BlockSpec(memory_space=pltpu.SMEM)
LAYOUT = ((0, (0, 1, 2, 3)), (-1, (0, 1, 2, 3)), (1, (0, 1, 2, 3)), (2, (0, 1)), (2, (2, 3)))
PIECES = len(LAYOUT)
PARAMS = pltpu.CompilerParams(vmem_limit_bytes=8 * 1024 * 1024)


def plane_pairs(by, last):
    pairs = []
    for x in range(SIDE):
        for y in range(SIDE):
            for c in range(2):
                along_x = (c == 0) == last
                to_x = (x + by) % SIDE if along_x else x
                to_y = y if along_x else (y + by) % SIDE
                pairs.append(((x * SIDE + y) * 2 + c, (to_x * SIDE + to_y) * 2 + c))
    return pairs


def shift(value, by, last):
    return lax.ppermute(value, PLANE, plane_pairs(by, last))


def swap(value):
    return lax.ppermute(value, "c", [(0, 1), (1, 0)])


def spread(piece):
    return [piece] + [shift(piece, by, False) for by in ORDER[1:]]


def relay(piece):
    behind, ahead = shift(piece, 1, True), shift(piece, SIDE - 1, True)
    return [piece, behind, ahead, shift(behind[:2], 1, True), shift(ahead[2:], SIDE - 1, True)]


def fold(own, up, down, far_up, far_down):
    from_behind, from_ahead = shift(far_up, 1, True), shift(far_down, SIDE - 1, True)
    up = jnp.concatenate([up[:2] + from_behind, up[2:]], 0)
    down = jnp.concatenate([down[:2], down[2:] + from_ahead], 0)
    from_behind, from_ahead = shift(up, 1, True), shift(down, SIDE - 1, True)
    return (own.astype(F32) + from_behind.astype(F32) + from_ahead.astype(F32)).astype(BF16)


def corner(me, away, j, thick, part):
    last = (me[1] + (away + SIDE)) % SIDE
    first = (me[2] + (SIDE - ORDER[j])) % SIDE
    row, column = jnp.where(me[0] == 0, first, last), jnp.where(me[0] == 0, last, first)
    return pl.multiple_of(row * thick, thick), pl.multiple_of(column * part, part)


def project_kernel(me, weight, extra, lift, *refs, centre):
    pieces, (laid, product) = refs[:PIECES], refs[-2:]
    thick, part = pieces[0].shape[1:]
    for piece, (away, blocks) in zip(pieces, LAYOUT):
        for i, j in enumerate(blocks):
            row, column = corner(me, away, j, thick, part)
            block = piece[i]
            if centre:
                block = (block.astype(F32) - extra[:, pl.ds(column, part)]).astype(BF16)
            laid[pl.ds(row, thick), pl.ds(column, part)] = block
    total = lift[...] if centre else None
    for q in range(SIDE):
        columns = pl.ds(q * part, part)
        term = lax.dot_general(
            laid[:, columns], weight[:, columns], (((1,), (1,)), ((), ())), preferred_element_type=F32
        )
        total = term if total is None else total + term
    product[...] = total


def project(me, weight, extra, lift, pieces, centre, after=()):
    thick, part = pieces[0].shape[1:]
    rows, width = thick * SIDE, part * SIDE
    args = (me, weight, extra, lift, *pieces, *after)
    return pl.pallas_call(
        functools.partial(project_kernel, centre=centre),
        out_shape=(jax.ShapeDtypeStruct((rows, width), BF16), jax.ShapeDtypeStruct((rows, weight.shape[0]), F32)),
        in_specs=[SMEM] + [VMEM] * (3 + PIECES) + [pl.BlockSpec(memory_space=pl.ANY)] * len(after),
        out_specs=(VMEM, VMEM),
        compiler_params=PARAMS,
        cost_estimate=pl.CostEstimate(
            flops=2 * rows * width * weight.shape[0], bytes_accessed=4 * rows * width, transcendentals=0
        ),
    )(*args)


def join(own, other, latents):
    return jnp.concatenate([own[:, :latents] + other[:, latents:], own[:, latents:] + other[:, :latents]], 1)


def recon_kernel(me, own, other, weight, preact, flat, *refs):
    blocks, (activity, laid) = refs[:PIECES], refs[PIECES:]
    _, thick, part = blocks[0].shape
    value = join(own[...], other[...], own.shape[1] // 2)
    preact[...] = value
    positive = jnp.maximum(value, 0.0)
    activity[...] = positive.astype(BF16)
    flat[...] = positive.T.astype(BF16)
    for q in range(SIDE):
        columns = pl.ds(q * part, part)
        laid[:, columns] = jnp.dot(activity[...], weight[:, columns], preferred_element_type=F32).astype(BF16)
    for piece, (away, wanted) in zip(blocks, LAYOUT):
        for i, j in enumerate(wanted):
            row, column = corner(me, -away, j, thick, part)
            piece[i] = laid[pl.ds(row, thick), pl.ds(column, part)]


def recon(me, own, other, weight):
    rows, wide = own.shape
    width = weight.shape[1]
    args = (me, own, other, weight)
    shapes = [jax.ShapeDtypeStruct((rows, wide), F32), jax.ShapeDtypeStruct((wide, rows), BF16)]
    for _, wanted in LAYOUT:
        shapes.append(jax.ShapeDtypeStruct((len(wanted), rows // SIDE, width // SIDE), BF16))
    return pl.pallas_call(
        recon_kernel,
        out_shape=tuple(shapes),
        in_specs=[SMEM] + [VMEM] * 3,
        out_specs=(VMEM,) * len(shapes),
        scratch_shapes=[pltpu.VMEM((rows, wide), BF16), pltpu.VMEM((rows, width), BF16)],
        compiler_params=PARAMS,
        cost_estimate=pl.CostEstimate(flops=2 * rows * wide * width, bytes_accessed=4 * rows * width, transcendentals=0),
    )(*args)


def error_kernel(me, parts, source, decoder, out):
    thin, part = out.shape[1:]
    x = jnp.where(me[0] == 0, me[1], me[2])
    rows = pl.ds(pl.multiple_of(me[3] * thin, thin), thin)
    value = jnp.sum(parts[...].astype(F32), 0) + decoder[:, pl.ds(pl.multiple_of(x * part, part), part)]
    value = (value - source[rows, :].astype(F32)).astype(BF16)
    for k in range(out.shape[0]):
        out[k] = value


def find_error(me, parts, source, decoder):
    return pl.pallas_call(
        error_kernel,
        out_shape=jax.ShapeDtypeStruct(parts.shape, BF16),
        in_specs=[SMEM] + [VMEM] * 3,
        out_specs=VMEM,
        compiler_params=PARAMS,
        cost_estimate=pl.CostEstimate(flops=10 * parts.size, bytes_accessed=4 * parts.size, transcendentals=0),
    )(me, parts, source, decoder)


def gradient_kernel(own, other, preact, flat, error, centered, *refs, chunk, final):
    slope = refs[-1]
    latents = preact.shape[1] // 2
    value = jnp.where(preact[...] > 0, join(own[...], other[...], latents), 0.0)
    slope[...] = value.T.astype(BF16)

    def step(j, carry):
        columns = pl.ds(pl.multiple_of(j * chunk, chunk), chunk)
        total = jnp.dot(flat[...], error[:, columns], preferred_element_type=F32)
        total += jnp.dot(slope[...], centered[:, columns], preferred_element_type=F32)
        if final:
            before, mine, theirs = refs[:3]
            total += before[:, columns]
            mine[:, columns] = total[:latents]
            theirs[:, columns] = total[latents:].astype(BF16)
        else:
            refs[0][:, columns] = total
        return carry

    lax.fori_loop(0, error.shape[1] // chunk, step, 0)


def gradient(args, before, chunk=1024):
    flat, error = args[3], args[4]
    wide, width = flat.shape[0], error.shape[1]
    if before is None:
        shapes = jax.ShapeDtypeStruct((wide, width), F32)
    else:
        args = args + (before,)
        shapes = (jax.ShapeDtypeStruct((wide // 2, width), F32), jax.ShapeDtypeStruct((wide // 2, width), BF16))
    return pl.pallas_call(
        functools.partial(gradient_kernel, chunk=chunk, final=before is not None),
        out_shape=shapes,
        in_specs=[VMEM] * len(args),
        out_specs=jax.tree.map(lambda _: VMEM, shapes),
        scratch_shapes=[pltpu.VMEM(flat.shape, BF16)],
        compiler_params=PARAMS,
        cost_estimate=pl.CostEstimate(flops=4 * flat.size * width, bytes_accessed=12 * error.size, transcendentals=0),
    )(*args)


def adam_kernel(at, gradient_ref, first_ref, second_ref, *refs, rows):
    update_out, first_out, second_out = refs[-3:]
    gradient = gradient_ref[...].astype(F32) * (1.0 / rows)
    first = 0.9 * first_ref[...].astype(F32) + 0.1 * gradient
    second = 0.999 * second_ref[...].astype(F32) + 0.001 * gradient * gradient
    update = first * (1.0 / (1.0 - 0.9**STEP)) / (jnp.sqrt(second * (1.0 / (1.0 - 0.999**STEP))) + 1e-08)
    update_out[...] = update.astype(BF16)
    first_out[...] = first.astype(BF16)
    second_out[...] = second.astype(BF16)


def adam(at, gradient, first_moment, second_moment, outs, rows, chunk=1024):
    latents, width = gradient.shape
    count = width // chunk
    here = pl.BlockSpec((latents, chunk), lambda i, at: (0, i))
    there = pl.BlockSpec((latents, chunk), lambda i, at: (0, at[0] * count + i))
    held = [pl.BlockSpec(memory_space=pl.ANY)] * len(outs)
    return pl.pallas_call(
        functools.partial(adam_kernel, rows=rows),
        out_shape=(jax.ShapeDtypeStruct(first_moment.shape, BF16),) * 3,
        grid_spec=pltpu.PrefetchScalarGridSpec(
            num_scalar_prefetch=1,
            grid=(count,),
            in_specs=[here, there, there] + held,
            out_specs=(there,) * 3,
        ),
        input_output_aliases={4 + i: i for i in range(len(outs))},
        compiler_params=PARAMS,
        cost_estimate=pl.CostEstimate(flops=20 * gradient.size, bytes_accessed=14 * gradient.size, transcendentals=0),
    )(at, gradient, first_moment, second_moment, *outs)


def body(inputs, dec_bias, weight, enc_bias, first_moment, second_moment):
    latents, width = weight.shape
    half = width // 2
    part = half // SIDE
    x, y, c = lax.axis_index("x"), lax.axis_index("y"), lax.axis_index("c")
    z = lax.axis_index(Z)
    last_me, first_me = jnp.where(c == 0, x, y), jnp.where(c == 0, y, x)
    me = jnp.stack([c, last_me, first_me, z]).astype(jnp.int32)

    own_columns = [lax.dynamic_slice_in_dim(inputs, core * half + x * part, part, 1) for core in range(2)]
    block = jnp.broadcast_to(jnp.stack(own_columns), (SIDE, 2) + own_columns[0].shape)
    block = lax.all_to_all(block.reshape((8,) + own_columns[0].shape), ("zh", "c"), 0, 0, tiled=True)
    block = block.reshape(-1, part)
    source = block
    split = source.shape[0] // CHUNKS
    gathered = spread(source)

    taken = swap(lax.dynamic_slice_in_dim(weight, (1 - c) * half, half, 1))
    pair = jnp.concatenate([lax.dynamic_slice_in_dim(weight, c * half, half, 1), taken], 0)
    decoder = lax.dynamic_slice_in_dim(dec_bias, c * half, half, 0)[None, :]
    lift = jnp.concatenate([enc_bias, jnp.zeros_like(enc_bias)])[None, :]
    rows = source.shape[0] * SIDE
    thin = source.shape[0] // 8

    def fan(gathered):
        return [relay(jnp.stack([g[k * split : (k + 1) * split] for g in gathered])) for k in chunks]

    chunks = range(CHUNKS)
    pieces = fan(gathered)
    ahead = [project(me, pair, decoder, lift, pieces[k], True) for k in chunks]
    made = [recon(me, ahead[k][1], swap(ahead[k][1]), pair) for k in chunks]
    blocks = jnp.concatenate([fold(*made[k][2:]) for k in chunks], 1)
    strip = blocks[0].astype(F32)
    for by in ORDER[1:]:
        strip = strip + shift(blocks[ORDER.index(SIDE - by)], by, False).astype(F32)
    parts = lax.all_to_all(strip.astype(BF16).reshape(8, thin, part), Z, 0, 0, tiled=True)
    error = find_error(me, parts, source, decoder)
    error = lax.all_to_all(error, Z, 0, 0, tiled=True)
    pieces = fan(spread(error.reshape(-1, part)))
    total = None
    for k in chunks:
        after = () if total is None else (total,)
        laid, own = project(me, pair, decoder, lift, pieces[k], False, after)
        total = gradient((own, swap(own), made[k][0], made[k][1], laid, ahead[k][0]), total)
    mine, theirs = total
    arrived = swap(theirs)
    at = c.astype(jnp.int32)[None]
    outs = adam(at, mine, first_moment, second_moment, (), rows)
    return tuple(adam(1 - at, arrived, first_moment, second_moment, outs, rows))


def solution(mesh):
    fine = Mesh(mesh.devices.reshape(4, 2, 4, 4, 2), ("x", "zl", "y", "zh", "c"))
    lat = ("y", "zh", "c")
    everything = ("x", "zl", "y", "zh", "c")
    return jax.shard_map(
        body,
        mesh=fine,
        in_specs=(P(lat, None), P(), P(everything, None), P(everything), P(everything, None), P(everything, None)),
        out_specs=(P(everything, None),) * 3,
        check_vma=False,
    )
```

```python
import functools

import jax
import jax.numpy as jnp
from jax import lax
from jax.experimental import pallas as pl
from jax.experimental.pallas import tpu as pltpu
from jax.sharding import Mesh, PartitionSpec as P

STEP = 100
BF16 = jnp.bfloat16
F32 = jnp.float32
SIDE = 4
CHUNKS = 2
ORDER = (0, 2, 1, 3)
PLANE = ("x", "y", "c")
Z = ("zh", "zl")
VMEM = pl.BlockSpec(memory_space=pltpu.VMEM)
SMEM = pl.BlockSpec(memory_space=pltpu.SMEM)
LAYOUT = ((0, (0, 1, 2, 3)), (-1, (0, 1, 2, 3)), (1, (0, 1, 2, 3)), (2, (0, 1)), (2, (2, 3)))
PIECES = len(LAYOUT)
WHOLE = tuple((-by, (0, 1, 2, 3)) for by in ORDER)
PARAMS = pltpu.CompilerParams(vmem_limit_bytes=8 * 1024 * 1024)


def plane_pairs(by, last):
    pairs = []
    for x in range(SIDE):
        for y in range(SIDE):
            for c in range(2):
                along_x = (c == 0) == last
                to_x = (x + by) % SIDE if along_x else x
                to_y = y if along_x else (y + by) % SIDE
                pairs.append(((x * SIDE + y) * 2 + c, (to_x * SIDE + to_y) * 2 + c))
    return pairs


def shift(value, by, last):
    return lax.ppermute(value, PLANE, plane_pairs(by, last))


def swap(value):
    return lax.ppermute(value, "c", [(0, 1), (1, 0)])


def spread(piece, last):
    return [piece] + [shift(piece, by, last) for by in ORDER[1:]]


def relay(piece):
    behind, ahead = shift(piece, 1, True), shift(piece, SIDE - 1, True)
    return [piece, behind, ahead, shift(behind[:2], 1, True), shift(ahead[2:], SIDE - 1, True)]


def fold(own, up, down, far_up, far_down):
    from_behind, from_ahead = shift(far_up, 1, True), shift(far_down, SIDE - 1, True)
    up = jnp.concatenate([up[:2] + from_behind, up[2:]], 0)
    down = jnp.concatenate([down[:2], down[2:] + from_ahead], 0)
    from_behind, from_ahead = shift(up, 1, True), shift(down, SIDE - 1, True)
    return (own.astype(F32) + from_behind.astype(F32) + from_ahead.astype(F32)).astype(BF16)


def corner(me, away, j, thick, part):
    last = (me[1] + (away + SIDE)) % SIDE
    first = (me[2] + (SIDE - ORDER[j])) % SIDE
    row, column = jnp.where(me[0] == 0, first, last), jnp.where(me[0] == 0, last, first)
    return pl.multiple_of(row * thick, thick), pl.multiple_of(column * part, part)


def project_kernel(me, weight, extra, lift, *refs, centre):
    layout = LAYOUT if centre else WHOLE
    pieces, (laid, product) = refs[: len(layout)], refs[-2:]
    thick, part = pieces[0].shape[1:]
    for piece, (away, blocks) in zip(pieces, layout):
        for i, j in enumerate(blocks):
            row, column = corner(me, away, j, thick, part)
            block = piece[i]
            if centre:
                block = (block.astype(F32) - extra[:, pl.ds(column, part)]).astype(BF16)
            laid[pl.ds(row, thick), pl.ds(column, part)] = block
    total = lift[...] if centre else None
    for q in range(SIDE):
        columns = pl.ds(q * part, part)
        term = lax.dot_general(
            laid[:, columns], weight[:, columns], (((1,), (1,)), ((), ())), preferred_element_type=F32
        )
        total = term if total is None else total + term
    product[...] = total


def project(me, weight, extra, lift, pieces, centre, after=()):
    thick, part = pieces[0].shape[1:]
    rows, width = thick * SIDE, part * SIDE
    args = (me, weight, extra, lift, *pieces, *after)
    return pl.pallas_call(
        functools.partial(project_kernel, centre=centre),
        out_shape=(jax.ShapeDtypeStruct((rows, width), BF16), jax.ShapeDtypeStruct((rows, weight.shape[0]), F32)),
        in_specs=[SMEM] + [VMEM] * (3 + len(pieces)) + [pl.BlockSpec(memory_space=pl.ANY)] * len(after),
        out_specs=(VMEM, VMEM),
        compiler_params=PARAMS,
        cost_estimate=pl.CostEstimate(
            flops=2 * rows * width * weight.shape[0], bytes_accessed=4 * rows * width, transcendentals=0
        ),
    )(*args)


def join(own, other, latents):
    return jnp.concatenate([own[:, :latents] + other[:, latents:], own[:, latents:] + other[:, :latents]], 1)


def recon_kernel(me, own, other, weight, preact, flat, *refs):
    blocks, (activity, laid) = refs[:PIECES], refs[PIECES:]
    _, thick, part = blocks[0].shape
    value = join(own[...], other[...], own.shape[1] // 2)
    preact[...] = value
    positive = jnp.maximum(value, 0.0)
    activity[...] = positive.astype(BF16)
    flat[...] = positive.T.astype(BF16)
    for q in range(SIDE):
        columns = pl.ds(q * part, part)
        laid[:, columns] = jnp.dot(activity[...], weight[:, columns], preferred_element_type=F32).astype(BF16)
    for piece, (away, wanted) in zip(blocks, LAYOUT):
        for i, j in enumerate(wanted):
            row, column = corner(me, -away, j, thick, part)
            piece[i] = laid[pl.ds(row, thick), pl.ds(column, part)]


def recon(me, own, other, weight):
    rows, wide = own.shape
    width = weight.shape[1]
    args = (me, own, other, weight)
    shapes = [jax.ShapeDtypeStruct((rows, wide), F32), jax.ShapeDtypeStruct((wide, rows), BF16)]
    for _, wanted in LAYOUT:
        shapes.append(jax.ShapeDtypeStruct((len(wanted), rows // SIDE, width // SIDE), BF16))
    return pl.pallas_call(
        recon_kernel,
        out_shape=tuple(shapes),
        in_specs=[SMEM] + [VMEM] * 3,
        out_specs=(VMEM,) * len(shapes),
        scratch_shapes=[pltpu.VMEM((rows, wide), BF16), pltpu.VMEM((rows, width), BF16)],
        compiler_params=PARAMS,
        cost_estimate=pl.CostEstimate(flops=2 * rows * wide * width, bytes_accessed=4 * rows * width, transcendentals=0),
    )(*args)


def error_kernel(me, parts, source, decoder, out):
    thin, part = out.shape[1:]
    x = jnp.where(me[0] == 0, me[1], me[2])
    rows = pl.ds(pl.multiple_of(me[3] * thin, thin), thin)
    value = jnp.sum(parts[...].astype(F32), 0) + decoder[:, pl.ds(pl.multiple_of(x * part, part), part)]
    value = (value - source[rows, :].astype(F32)).astype(BF16)
    for k in range(out.shape[0]):
        out[k] = value


def find_error(me, parts, source, decoder):
    return pl.pallas_call(
        error_kernel,
        out_shape=jax.ShapeDtypeStruct(parts.shape, BF16),
        in_specs=[SMEM] + [VMEM] * 3,
        out_specs=VMEM,
        compiler_params=PARAMS,
        cost_estimate=pl.CostEstimate(flops=10 * parts.size, bytes_accessed=4 * parts.size, transcendentals=0),
    )(me, parts, source, decoder)


def gradient_kernel(own, other, preact, flat, error, centered, *refs, chunk, final):
    slope = refs[-1]
    latents = preact.shape[1] // 2
    value = jnp.where(preact[...] > 0, join(own[...], other[...], latents), 0.0)
    slope[...] = value.T.astype(BF16)

    def step(j, carry):
        columns = pl.ds(pl.multiple_of(j * chunk, chunk), chunk)
        total = jnp.dot(flat[...], error[:, columns], preferred_element_type=F32)
        total += jnp.dot(slope[...], centered[:, columns], preferred_element_type=F32)
        if final:
            before, mine, theirs = refs[:3]
            total += before[:, columns]
            mine[:, columns] = total[:latents]
            theirs[:, columns] = total[latents:].astype(BF16)
        else:
            refs[0][:, columns] = total
        return carry

    lax.fori_loop(0, error.shape[1] // chunk, step, 0)


def gradient(args, before, chunk=1024):
    flat, error = args[3], args[4]
    wide, width = flat.shape[0], error.shape[1]
    if before is None:
        shapes = jax.ShapeDtypeStruct((wide, width), F32)
    else:
        args = args + (before,)
        shapes = (jax.ShapeDtypeStruct((wide // 2, width), F32), jax.ShapeDtypeStruct((wide // 2, width), BF16))
    return pl.pallas_call(
        functools.partial(gradient_kernel, chunk=chunk, final=before is not None),
        out_shape=shapes,
        in_specs=[VMEM] * len(args),
        out_specs=jax.tree.map(lambda _: VMEM, shapes),
        scratch_shapes=[pltpu.VMEM(flat.shape, BF16)],
        compiler_params=PARAMS,
        cost_estimate=pl.CostEstimate(flops=4 * flat.size * width, bytes_accessed=12 * error.size, transcendentals=0),
    )(*args)


def adam_kernel(at, gradient_ref, first_ref, second_ref, *refs, rows):
    update_out, first_out, second_out = refs[-3:]
    gradient = gradient_ref[...].astype(F32) * (1.0 / rows)
    first = 0.9 * first_ref[...].astype(F32) + 0.1 * gradient
    second = 0.999 * second_ref[...].astype(F32) + 0.001 * gradient * gradient
    update = first * (1.0 / (1.0 - 0.9**STEP)) / (jnp.sqrt(second * (1.0 / (1.0 - 0.999**STEP))) + 1e-08)
    update_out[...] = update.astype(BF16)
    first_out[...] = first.astype(BF16)
    second_out[...] = second.astype(BF16)


def adam(at, gradient, first_moment, second_moment, outs, rows, chunk=1024):
    latents, width = gradient.shape
    count = width // chunk
    here = pl.BlockSpec((latents, chunk), lambda i, at: (0, i))
    there = pl.BlockSpec((latents, chunk), lambda i, at: (0, at[0] * count + i))
    held = [pl.BlockSpec(memory_space=pl.ANY)] * len(outs)
    return pl.pallas_call(
        functools.partial(adam_kernel, rows=rows),
        out_shape=(jax.ShapeDtypeStruct(first_moment.shape, BF16),) * 3,
        grid_spec=pltpu.PrefetchScalarGridSpec(
            num_scalar_prefetch=1,
            grid=(count,),
            in_specs=[here, there, there] + held,
            out_specs=(there,) * 3,
        ),
        input_output_aliases={4 + i: i for i in range(len(outs))},
        compiler_params=PARAMS,
        cost_estimate=pl.CostEstimate(flops=20 * gradient.size, bytes_accessed=14 * gradient.size, transcendentals=0),
    )(at, gradient, first_moment, second_moment, *outs)


def body(inputs, dec_bias, weight, enc_bias, first_moment, second_moment):
    latents, width = weight.shape
    half = width // 2
    part = half // SIDE
    x, y, c = lax.axis_index("x"), lax.axis_index("y"), lax.axis_index("c")
    zh, z = lax.axis_index("zh"), lax.axis_index(Z)
    last_me, first_me = jnp.where(c == 0, x, y), jnp.where(c == 0, y, x)
    me = jnp.stack([c, last_me, first_me, z]).astype(jnp.int32)

    kept = lax.dynamic_slice_in_dim(inputs, c * half + x * part, part, 1)
    given = swap(lax.dynamic_slice_in_dim(inputs, (1 - c) * half + x * part, part, 1))
    both = jnp.concatenate([jnp.where(c == 0, kept, given), jnp.where(c == 0, given, kept)], 0)
    count = both.shape[0]
    block = lax.dynamic_update_slice_in_dim(jnp.zeros((SIDE * count, part), BF16), both, zh * count, 0)
    for by in ORDER[1:]:
        arrived = lax.ppermute(both, "zh", [(i, (i + by) % SIDE) for i in range(SIDE)])
        block = lax.dynamic_update_slice_in_dim(block, arrived, (zh - by) % SIDE * count, 0)
    source = block
    split = source.shape[0] // CHUNKS
    gathered = spread(source, False)

    pair = jnp.concatenate(
        [lax.dynamic_slice_in_dim(rows_held, c * half, half, 1) for rows_held in (weight, swap(weight))], 0
    )
    decoder = lax.dynamic_slice_in_dim(dec_bias, c * half, half, 0)[None, :]
    lift = jnp.concatenate([enc_bias, jnp.zeros_like(enc_bias)])[None, :]
    rows = source.shape[0] * SIDE
    thin = source.shape[0] // 8

    def fan(gathered, send):
        return [send(jnp.stack([g[k * split : (k + 1) * split] for g in gathered])) for k in chunks]

    chunks = range(CHUNKS)
    pieces = fan(gathered, relay)
    ahead, made = [], []
    for k in chunks:
        ahead.append(project(me, pair, decoder, lift, pieces[k], True))
        made.append(recon(me, ahead[k][1], swap(ahead[k][1]), pair))
    blocks = jnp.concatenate([fold(*made[k][2:]) for k in chunks], 1)
    strip = blocks[0].astype(F32)
    for by in ORDER[1:]:
        strip = strip + shift(blocks[ORDER.index(SIDE - by)], by, False).astype(F32)
    parts = lax.all_to_all(strip.astype(BF16).reshape(8, thin, part), Z, 0, 0, tiled=True)
    error = find_error(me, parts, source, decoder)
    error = lax.all_to_all(error, Z, 0, 0, tiled=True)
    pieces = fan(spread(error.reshape(-1, part), False), lambda piece: spread(piece, True))
    total = None
    for k in chunks:
        after = () if total is None else (total,)
        laid, own = project(me, pair, decoder, lift, pieces[k], False, after)
        total = gradient((own, swap(own), made[k][0], made[k][1], laid, ahead[k][0]), total)
    mine, theirs = total
    arrived = swap(theirs)
    at = c.astype(jnp.int32)[None]
    outs = adam(at, mine, first_moment, second_moment, (), rows)
    return tuple(adam(1 - at, arrived, first_moment, second_moment, outs, rows))


def solution(mesh):
    fine = Mesh(mesh.devices.reshape(4, 2, 4, 4, 2), ("x", "zl", "y", "zh", "c"))
    lat = ("y", "zh", "c")
    everything = ("x", "zl", "y", "zh", "c")
    return jax.shard_map(
        body,
        mesh=fine,
        in_specs=(P(lat, None), P(), P(everything, None), P(everything), P(everything, None), P(everything, None)),
        out_specs=(P(everything, None),) * 3,
        check_vma=False,
    )
```

```python
import functools

import jax
import jax.numpy as jnp
from jax import lax
from jax.experimental import pallas as pl
from jax.experimental.pallas import tpu as pltpu
from jax.sharding import Mesh, PartitionSpec as P

STEP = 100
BF16 = jnp.bfloat16
F32 = jnp.float32
SIDE = 4
CHUNKS = 2
ORDER = (0, 2, 1, 3)
PLANE = ("x", "y", "c")
Z = ("zh", "zl")
VMEM = pl.BlockSpec(memory_space=pltpu.VMEM)
SMEM = pl.BlockSpec(memory_space=pltpu.SMEM)
LAYOUT = ((0, (0, 1, 2, 3)), (-1, (0, 1, 2, 3)), (1, (0, 1, 2, 3)), (2, (0, 1)), (2, (2, 3)))
PIECES = len(LAYOUT)
WHOLE = tuple((-by, (0, 1, 2, 3)) for by in ORDER)
PARAMS = pltpu.CompilerParams(vmem_limit_bytes=8 * 1024 * 1024)


def plane_pairs(by, last):
    pairs = []
    for x in range(SIDE):
        for y in range(SIDE):
            for c in range(2):
                along_x = (c == 0) == last
                to_x = (x + by) % SIDE if along_x else x
                to_y = y if along_x else (y + by) % SIDE
                pairs.append(((x * SIDE + y) * 2 + c, (to_x * SIDE + to_y) * 2 + c))
    return pairs


def shift(value, by, last):
    return lax.ppermute(value, PLANE, plane_pairs(by, last))


def swap(value):
    return lax.ppermute(value, "c", [(0, 1), (1, 0)])


def spread(piece, last):
    return [piece] + [shift(piece, by, last) for by in ORDER[1:]]


def relay(piece):
    behind, ahead = shift(piece, 1, True), shift(piece, SIDE - 1, True)
    return [piece, behind, ahead, shift(behind[:2], 1, True), shift(ahead[2:], SIDE - 1, True)]


def fold(own, up, down, far_up, far_down):
    from_behind, from_ahead = shift(far_up, 1, True), shift(far_down, SIDE - 1, True)
    up = jnp.concatenate([up[:2] + from_behind, up[2:]], 0)
    down = jnp.concatenate([down[:2], down[2:] + from_ahead], 0)
    from_behind, from_ahead = shift(up, 1, True), shift(down, SIDE - 1, True)
    return (own.astype(F32) + from_behind.astype(F32) + from_ahead.astype(F32)).astype(BF16)


def corner(me, away, j, thick, part):
    last = (me[1] + (away + SIDE)) % SIDE
    first = (me[2] + (SIDE - (j % 2 * 2 + j // 2))) % SIDE
    row, column = jnp.where(me[0] == 0, first, last), jnp.where(me[0] == 0, last, first)
    return pl.multiple_of(row * thick, thick), pl.multiple_of(column * part, part)


def project_kernel(me, weight, extra, lift, *refs, centre):
    layout = LAYOUT if centre else WHOLE
    pieces, (laid, product) = refs[: len(layout)], refs[-2:]
    thick, part = pieces[0].shape[1:]
    for piece, (away, blocks) in zip(pieces, layout):

        def place(i, carry, piece=piece, away=away, begin=blocks[0]):
            row, column = corner(me, away, begin + i, thick, part)
            block = piece[i]
            if centre:
                block = (block.astype(F32) - extra[:, pl.ds(column, part)]).astype(BF16)
            laid[pl.ds(row, thick), pl.ds(column, part)] = block
            return carry

        lax.fori_loop(0, len(blocks), place, 0)
    product[...] = jnp.broadcast_to(lift[...], product.shape) if centre else jnp.zeros_like(product)

    def multiply(q, carry):
        columns = pl.ds(pl.multiple_of(q * part, part), part)
        product[...] += lax.dot_general(
            laid[:, columns], weight[:, columns], (((1,), (1,)), ((), ())), preferred_element_type=F32
        )
        return carry

    lax.fori_loop(0, SIDE, multiply, 0)


def project(me, weight, extra, lift, pieces, centre, after=()):
    thick, part = pieces[0].shape[1:]
    rows, width = thick * SIDE, part * SIDE
    args = (me, weight, extra, lift, *pieces, *after)
    return pl.pallas_call(
        functools.partial(project_kernel, centre=centre),
        out_shape=(jax.ShapeDtypeStruct((rows, width), BF16), jax.ShapeDtypeStruct((rows, weight.shape[0]), F32)),
        in_specs=[SMEM] + [VMEM] * (3 + len(pieces)) + [pl.BlockSpec(memory_space=pl.ANY)] * len(after),
        out_specs=(VMEM, VMEM),
        compiler_params=PARAMS,
        cost_estimate=pl.CostEstimate(
            flops=2 * rows * width * weight.shape[0], bytes_accessed=4 * rows * width, transcendentals=0
        ),
    )(*args)


def join(own, other, latents):
    return jnp.concatenate([own[:, :latents] + other[:, latents:], own[:, latents:] + other[:, :latents]], 1)


def recon_kernel(me, own, other, weight, preact, flat, *refs):
    blocks, (activity, laid) = refs[:PIECES], refs[PIECES:]
    _, thick, part = blocks[0].shape
    value = join(own[...], other[...], own.shape[1] // 2)
    preact[...] = value
    positive = jnp.maximum(value, 0.0)
    activity[...] = positive.astype(BF16)
    flat[...] = positive.T.astype(BF16)

    def multiply(q, carry):
        columns = pl.ds(pl.multiple_of(q * part, part), part)
        laid[:, columns] = jnp.dot(activity[...], weight[:, columns], preferred_element_type=F32).astype(BF16)
        return carry

    lax.fori_loop(0, SIDE, multiply, 0)
    for piece, (away, wanted) in zip(blocks, LAYOUT):

        def take(i, carry, piece=piece, away=away, begin=wanted[0]):
            row, column = corner(me, -away, begin + i, thick, part)
            piece[i] = laid[pl.ds(row, thick), pl.ds(column, part)]
            return carry

        lax.fori_loop(0, len(wanted), take, 0)


def recon(me, own, other, weight):
    rows, wide = own.shape
    width = weight.shape[1]
    args = (me, own, other, weight)
    shapes = [jax.ShapeDtypeStruct((rows, wide), F32), jax.ShapeDtypeStruct((wide, rows), BF16)]
    for _, wanted in LAYOUT:
        shapes.append(jax.ShapeDtypeStruct((len(wanted), rows // SIDE, width // SIDE), BF16))
    return pl.pallas_call(
        recon_kernel,
        out_shape=tuple(shapes),
        in_specs=[SMEM] + [VMEM] * 3,
        out_specs=(VMEM,) * len(shapes),
        scratch_shapes=[pltpu.VMEM((rows, wide), BF16), pltpu.VMEM((rows, width), BF16)],
        compiler_params=PARAMS,
        cost_estimate=pl.CostEstimate(flops=2 * rows * wide * width, bytes_accessed=4 * rows * width, transcendentals=0),
    )(*args)


def error_kernel(me, parts, source, decoder, out):
    thin, part = out.shape[1:]
    x = jnp.where(me[0] == 0, me[1], me[2])
    rows = pl.ds(pl.multiple_of(me[3] * thin, thin), thin)
    value = jnp.sum(parts[...].astype(F32), 0) + decoder[:, pl.ds(pl.multiple_of(x * part, part), part)]
    value = (value - source[rows, :].astype(F32)).astype(BF16)
    for k in range(out.shape[0]):
        out[k] = value


def find_error(me, parts, source, decoder):
    return pl.pallas_call(
        error_kernel,
        out_shape=jax.ShapeDtypeStruct(parts.shape, BF16),
        in_specs=[SMEM] + [VMEM] * 3,
        out_specs=VMEM,
        compiler_params=PARAMS,
        cost_estimate=pl.CostEstimate(flops=10 * parts.size, bytes_accessed=4 * parts.size, transcendentals=0),
    )(me, parts, source, decoder)


def gradient_kernel(own, other, preact, flat, error, centered, *refs, chunk, final):
    slope = refs[-1]
    latents = preact.shape[1] // 2
    value = jnp.where(preact[...] > 0, join(own[...], other[...], latents), 0.0)
    slope[...] = value.T.astype(BF16)

    def step(j, carry):
        columns = pl.ds(pl.multiple_of(j * chunk, chunk), chunk)
        total = jnp.dot(flat[...], error[:, columns], preferred_element_type=F32)
        total += jnp.dot(slope[...], centered[:, columns], preferred_element_type=F32)
        if final:
            before, mine, theirs = refs[:3]
            total += before[:, columns]
            mine[:, columns] = total[:latents]
            theirs[:, columns] = total[latents:].astype(BF16)
        else:
            refs[0][:, columns] = total
        return carry

    lax.fori_loop(0, error.shape[1] // chunk, step, 0)


def gradient(args, before, chunk=1024):
    flat, error = args[3], args[4]
    wide, width = flat.shape[0], error.shape[1]
    if before is None:
        shapes = jax.ShapeDtypeStruct((wide, width), F32)
    else:
        args = args + (before,)
        shapes = (jax.ShapeDtypeStruct((wide // 2, width), F32), jax.ShapeDtypeStruct((wide // 2, width), BF16))
    return pl.pallas_call(
        functools.partial(gradient_kernel, chunk=chunk, final=before is not None),
        out_shape=shapes,
        in_specs=[VMEM] * len(args),
        out_specs=jax.tree.map(lambda _: VMEM, shapes),
        scratch_shapes=[pltpu.VMEM(flat.shape, BF16)],
        compiler_params=PARAMS,
        cost_estimate=pl.CostEstimate(flops=4 * flat.size * width, bytes_accessed=12 * error.size, transcendentals=0),
    )(*args)


def adam_kernel(at, gradient_ref, first_ref, second_ref, *refs, rows):
    update_out, first_out, second_out = refs[-3:]
    gradient = gradient_ref[...].astype(F32) * (1.0 / rows)
    first = 0.9 * first_ref[...].astype(F32) + 0.1 * gradient
    second = 0.999 * second_ref[...].astype(F32) + 0.001 * gradient * gradient
    update = first * (1.0 / (1.0 - 0.9**STEP)) / (jnp.sqrt(second * (1.0 / (1.0 - 0.999**STEP))) + 1e-08)
    update_out[...] = update.astype(BF16)
    first_out[...] = first.astype(BF16)
    second_out[...] = second.astype(BF16)


def adam(at, gradient, first_moment, second_moment, outs, rows, chunk=1024):
    latents, width = gradient.shape
    count = width // chunk
    here = pl.BlockSpec((latents, chunk), lambda i, at: (0, i))
    there = pl.BlockSpec((latents, chunk), lambda i, at: (0, at[0] * count + i))
    held = [pl.BlockSpec(memory_space=pl.ANY)] * len(outs)
    return pl.pallas_call(
        functools.partial(adam_kernel, rows=rows),
        out_shape=(jax.ShapeDtypeStruct(first_moment.shape, BF16),) * 3,
        grid_spec=pltpu.PrefetchScalarGridSpec(
            num_scalar_prefetch=1,
            grid=(count,),
            in_specs=[here, there, there] + held,
            out_specs=(there,) * 3,
        ),
        input_output_aliases={4 + i: i for i in range(len(outs))},
        compiler_params=PARAMS,
        cost_estimate=pl.CostEstimate(flops=20 * gradient.size, bytes_accessed=14 * gradient.size, transcendentals=0),
    )(at, gradient, first_moment, second_moment, *outs)


def body(inputs, dec_bias, weight, enc_bias, first_moment, second_moment):
    latents, width = weight.shape
    half = width // 2
    part = half // SIDE
    x, y, c = lax.axis_index("x"), lax.axis_index("y"), lax.axis_index("c")
    zh, z = lax.axis_index("zh"), lax.axis_index(Z)
    last_me, first_me = jnp.where(c == 0, x, y), jnp.where(c == 0, y, x)
    me = jnp.stack([c, last_me, first_me, z]).astype(jnp.int32)

    kept = lax.dynamic_slice_in_dim(inputs, c * half + x * part, part, 1)
    given = swap(lax.dynamic_slice_in_dim(inputs, (1 - c) * half + x * part, part, 1))
    both = jnp.concatenate([jnp.where(c == 0, kept, given), jnp.where(c == 0, given, kept)], 0)
    count = both.shape[0]
    block = lax.dynamic_update_slice_in_dim(jnp.zeros((SIDE * count, part), BF16), both, zh * count, 0)
    for by in ORDER[1:]:
        arrived = lax.ppermute(both, "zh", [(i, (i + by) % SIDE) for i in range(SIDE)])
        block = lax.dynamic_update_slice_in_dim(block, arrived, (zh - by) % SIDE * count, 0)
    source = block
    split = source.shape[0] // CHUNKS
    gathered = spread(source, False)

    pair = jnp.concatenate(
        [lax.dynamic_slice_in_dim(rows_held, c * half, half, 1) for rows_held in (weight, swap(weight))], 0
    )
    decoder = lax.dynamic_slice_in_dim(dec_bias, c * half, half, 0)[None, :]
    lift = jnp.concatenate([enc_bias, jnp.zeros_like(enc_bias)])[None, :]
    rows = source.shape[0] * SIDE
    thin = source.shape[0] // 8

    def fan(gathered, send):
        return [send(jnp.stack([g[k * split : (k + 1) * split] for g in gathered])) for k in chunks]

    chunks = range(CHUNKS)
    pieces = fan(gathered, relay)
    ahead, made = [], []
    for k in chunks:
        ahead.append(project(me, pair, decoder, lift, pieces[k], True))
        made.append(recon(me, ahead[k][1], swap(ahead[k][1]), pair))
    blocks = jnp.concatenate([fold(*made[k][2:]) for k in chunks], 1)
    strip = blocks[0].astype(F32)
    for by in ORDER[1:]:
        strip = strip + shift(blocks[ORDER.index(SIDE - by)], by, False).astype(F32)
    parts = lax.all_to_all(strip.astype(BF16).reshape(8, thin, part), Z, 0, 0, tiled=True)
    error = find_error(me, parts, source, decoder)
    error = lax.all_to_all(error, Z, 0, 0, tiled=True)
    pieces = fan(spread(error.reshape(-1, part), False), lambda piece: spread(piece, True))
    total = None
    for k in chunks:
        after = () if total is None else (total,)
        laid, own = project(me, pair, decoder, lift, pieces[k], False, after)
        total = gradient((own, swap(own), made[k][0], made[k][1], laid, ahead[k][0]), total)
    mine, theirs = total
    arrived = swap(theirs)
    at = c.astype(jnp.int32)[None]
    outs = adam(at, mine, first_moment, second_moment, (), rows)
    return tuple(adam(1 - at, arrived, first_moment, second_moment, outs, rows))


def solution(mesh):
    fine = Mesh(mesh.devices.reshape(4, 2, 4, 4, 2), ("x", "zl", "y", "zh", "c"))
    lat = ("y", "zh", "c")
    everything = ("x", "zl", "y", "zh", "c")
    return jax.shard_map(
        body,
        mesh=fine,
        in_specs=(P(lat, None), P(), P(everything, None), P(everything), P(everything, None), P(everything, None)),
        out_specs=(P(everything, None),) * 3,
        check_vma=False,
    )
```

```python
import functools

import jax
import jax.numpy as jnp
from jax import lax
from jax.experimental import pallas as pl
from jax.experimental.pallas import tpu as pltpu
from jax.sharding import Mesh, PartitionSpec as P

STEP = 100
BF16 = jnp.bfloat16
F32 = jnp.float32
SIDE = 4
CHUNKS = 2
ORDER = (0, 2, 1, 3)
PLANE = ("x", "y", "c")
Z = ("zh", "zl")
VMEM = pl.BlockSpec(memory_space=pltpu.VMEM)
SMEM = pl.BlockSpec(memory_space=pltpu.SMEM)
LAYOUT = ((0, (0, 1, 2, 3)), (-1, (0, 1, 2, 3)), (1, (0, 1, 2, 3)), (2, (0, 1)), (2, (2, 3)))
PIECES = len(LAYOUT)
WHOLE = tuple((-by, (0, 1, 2, 3)) for by in ORDER)
PARAMS = pltpu.CompilerParams(vmem_limit_bytes=8 * 1024 * 1024)


def plane_pairs(by, last):
    pairs = []
    for x in range(SIDE):
        for y in range(SIDE):
            for c in range(2):
                along_x = (c == 0) == last
                to_x = (x + by) % SIDE if along_x else x
                to_y = y if along_x else (y + by) % SIDE
                pairs.append(((x * SIDE + y) * 2 + c, (to_x * SIDE + to_y) * 2 + c))
    return pairs


def shift(value, by, last):
    return lax.ppermute(value, PLANE, plane_pairs(by, last))


def swap(value):
    return lax.ppermute(value, "c", [(0, 1), (1, 0)])


def spread(piece, last):
    return [piece] + [shift(piece, by, last) for by in ORDER[1:]]


def relay(piece):
    behind, ahead = shift(piece, 1, True), shift(piece, SIDE - 1, True)
    return [piece, behind, ahead, shift(behind[:2], 1, True), shift(ahead[2:], SIDE - 1, True)]


def fold(own, up, down, far_up, far_down):
    from_behind, from_ahead = shift(far_up, 1, True), shift(far_down, SIDE - 1, True)
    up = jnp.concatenate([up[:2] + from_behind, up[2:]], 0)
    down = jnp.concatenate([down[:2], down[2:] + from_ahead], 0)
    from_behind, from_ahead = shift(up, 1, True), shift(down, SIDE - 1, True)
    return (own.astype(F32) + from_behind.astype(F32) + from_ahead.astype(F32)).astype(BF16)


def corner(me, away, j, thick, part):
    last = (me[1] + (away + SIDE)) % SIDE
    first = (me[2] + (SIDE - (j % 2 * 2 + j // 2))) % SIDE
    row, column = jnp.where(me[0] == 0, first, last), jnp.where(me[0] == 0, last, first)
    return pl.multiple_of(row * thick, thick), pl.multiple_of(column * part, part)


def project_kernel(me, weight, extra, lift, *refs, centre, looped):
    layout = LAYOUT if centre else WHOLE
    pieces, (laid, product) = refs[: len(layout)], refs[-2:]
    thick, part = pieces[0].shape[1:]
    for piece, (away, blocks) in zip(pieces, layout):

        def place(i, carry, piece=piece, away=away, begin=blocks[0]):
            row, column = corner(me, away, begin + i, thick, part)
            block = piece[i]
            if centre:
                block = (block.astype(F32) - extra[:, pl.ds(column, part)]).astype(BF16)
            laid[pl.ds(row, thick), pl.ds(column, part)] = block
            return carry

        lax.fori_loop(0, len(blocks), place, 0)

    def term(columns):
        return lax.dot_general(
            laid[:, columns], weight[:, columns], (((1,), (1,)), ((), ())), preferred_element_type=F32
        )

    def add(q, carry):
        product[...] += term(pl.ds(pl.multiple_of(q * part, part), part))
        return carry

    if looped:
        product[...] = term(pl.ds(0, part))
        lax.fori_loop(1, SIDE, add, 0)
    else:
        total = lift[...] if centre else None
        for q in range(SIDE):
            total = term(pl.ds(q * part, part)) if total is None else total + term(pl.ds(q * part, part))
        product[...] = total


def project(me, weight, extra, lift, pieces, centre, after=(), looped=False):
    thick, part = pieces[0].shape[1:]
    rows, width = thick * SIDE, part * SIDE
    args = (me, weight, extra, lift, *pieces, *after)
    return pl.pallas_call(
        functools.partial(project_kernel, centre=centre, looped=looped),
        out_shape=(jax.ShapeDtypeStruct((rows, width), BF16), jax.ShapeDtypeStruct((rows, weight.shape[0]), F32)),
        in_specs=[SMEM] + [VMEM] * (3 + len(pieces)) + [pl.BlockSpec(memory_space=pl.ANY)] * len(after),
        out_specs=(VMEM, VMEM),
        compiler_params=PARAMS,
        cost_estimate=pl.CostEstimate(
            flops=2 * rows * width * weight.shape[0], bytes_accessed=4 * rows * width, transcendentals=0
        ),
    )(*args)


def join(own, other, latents):
    return jnp.concatenate([own[:, :latents] + other[:, latents:], own[:, latents:] + other[:, :latents]], 1)


def recon_kernel(me, own, other, weight, preact, flat, *refs, looped):
    blocks, (activity, laid) = refs[:PIECES], refs[PIECES:]
    _, thick, part = blocks[0].shape
    value = join(own[...], other[...], own.shape[1] // 2)
    preact[...] = value
    positive = jnp.maximum(value, 0.0)
    activity[...] = positive.astype(BF16)
    flat[...] = positive.T.astype(BF16)

    def multiply(q, carry):
        columns = pl.ds(pl.multiple_of(q * part, part), part)
        laid[:, columns] = jnp.dot(activity[...], weight[:, columns], preferred_element_type=F32).astype(BF16)
        return carry

    lax.fori_loop(0, SIDE, multiply, 0, unroll=not looped)
    for piece, (away, wanted) in zip(blocks, LAYOUT):

        def take(i, carry, piece=piece, away=away, begin=wanted[0]):
            row, column = corner(me, -away, begin + i, thick, part)
            piece[i] = laid[pl.ds(row, thick), pl.ds(column, part)]
            return carry

        lax.fori_loop(0, len(wanted), take, 0)


def recon(me, own, other, weight, looped):
    rows, wide = own.shape
    width = weight.shape[1]
    args = (me, own, other, weight)
    shapes = [jax.ShapeDtypeStruct((rows, wide), F32), jax.ShapeDtypeStruct((wide, rows), BF16)]
    for _, wanted in LAYOUT:
        shapes.append(jax.ShapeDtypeStruct((len(wanted), rows // SIDE, width // SIDE), BF16))
    return pl.pallas_call(
        functools.partial(recon_kernel, looped=looped),
        out_shape=tuple(shapes),
        in_specs=[SMEM] + [VMEM] * 3,
        out_specs=(VMEM,) * len(shapes),
        scratch_shapes=[pltpu.VMEM((rows, wide), BF16), pltpu.VMEM((rows, width), BF16)],
        compiler_params=PARAMS,
        cost_estimate=pl.CostEstimate(flops=2 * rows * wide * width, bytes_accessed=4 * rows * width, transcendentals=0),
    )(*args)


def error_kernel(me, parts, source, decoder, out):
    thin, part = out.shape[1:]
    x = jnp.where(me[0] == 0, me[1], me[2])
    rows = pl.ds(pl.multiple_of(me[3] * thin, thin), thin)
    value = jnp.sum(parts[...].astype(F32), 0) + decoder[:, pl.ds(pl.multiple_of(x * part, part), part)]
    value = (value - source[rows, :].astype(F32)).astype(BF16)
    for k in range(out.shape[0]):
        out[k] = value


def find_error(me, parts, source, decoder):
    return pl.pallas_call(
        error_kernel,
        out_shape=jax.ShapeDtypeStruct(parts.shape, BF16),
        in_specs=[SMEM] + [VMEM] * 3,
        out_specs=VMEM,
        compiler_params=PARAMS,
        cost_estimate=pl.CostEstimate(flops=10 * parts.size, bytes_accessed=4 * parts.size, transcendentals=0),
    )(me, parts, source, decoder)


def gradient_kernel(own, other, preact, flat, error, centered, *refs, chunk, final):
    slope = refs[-1]
    latents = preact.shape[1] // 2
    value = jnp.where(preact[...] > 0, join(own[...], other[...], latents), 0.0)
    slope[...] = value.T.astype(BF16)

    def step(j, carry):
        columns = pl.ds(pl.multiple_of(j * chunk, chunk), chunk)
        total = jnp.dot(flat[...], error[:, columns], preferred_element_type=F32)
        total += jnp.dot(slope[...], centered[:, columns], preferred_element_type=F32)
        if final:
            before, mine, theirs = refs[:3]
            total += before[:, columns]
            mine[:, columns] = total[:latents]
            theirs[:, columns] = total[latents:].astype(BF16)
        else:
            refs[0][:, columns] = total
        return carry

    lax.fori_loop(0, error.shape[1] // chunk, step, 0)


def gradient(args, before):
    chunk = 512 if before is None else 1024
    flat, error = args[3], args[4]
    wide, width = flat.shape[0], error.shape[1]
    if before is None:
        shapes = jax.ShapeDtypeStruct((wide, width), F32)
    else:
        args = args + (before,)
        shapes = (jax.ShapeDtypeStruct((wide // 2, width), F32), jax.ShapeDtypeStruct((wide // 2, width), BF16))
    return pl.pallas_call(
        functools.partial(gradient_kernel, chunk=chunk, final=before is not None),
        out_shape=shapes,
        in_specs=[VMEM] * len(args),
        out_specs=jax.tree.map(lambda _: VMEM, shapes),
        scratch_shapes=[pltpu.VMEM(flat.shape, BF16)],
        compiler_params=PARAMS,
        cost_estimate=pl.CostEstimate(flops=4 * flat.size * width, bytes_accessed=12 * error.size, transcendentals=0),
    )(*args)


def adam_kernel(at, gradient_ref, first_ref, second_ref, *refs, rows):
    update_out, first_out, second_out = refs[-3:]
    strip = 16

    def step(i, carry):
        here = pl.ds(pl.multiple_of(i * strip, strip), strip)
        gradient = gradient_ref[here, :].astype(F32) * (1.0 / rows)
        first = 0.9 * first_ref[here, :].astype(F32) + 0.1 * gradient
        second = 0.999 * second_ref[here, :].astype(F32) + 0.001 * gradient * gradient
        update = first * (1.0 / (1.0 - 0.9**STEP)) / (jnp.sqrt(second * (1.0 / (1.0 - 0.999**STEP))) + 1e-08)
        update_out[here, :] = update.astype(BF16)
        first_out[here, :] = first.astype(BF16)
        second_out[here, :] = second.astype(BF16)
        return carry

    lax.fori_loop(0, gradient_ref.shape[0] // strip, step, 0)


def adam(at, gradient, first_moment, second_moment, outs, rows, chunk=1024):
    latents, width = gradient.shape
    count = width // chunk
    here = pl.BlockSpec((latents, chunk), lambda i, at: (0, i))
    there = pl.BlockSpec((latents, chunk), lambda i, at: (0, at[0] * count + i))
    held = [pl.BlockSpec(memory_space=pl.ANY)] * len(outs)
    return pl.pallas_call(
        functools.partial(adam_kernel, rows=rows),
        out_shape=(jax.ShapeDtypeStruct(first_moment.shape, BF16),) * 3,
        grid_spec=pltpu.PrefetchScalarGridSpec(
            num_scalar_prefetch=1,
            grid=(count,),
            in_specs=[here, there, there] + held,
            out_specs=(there,) * 3,
        ),
        input_output_aliases={4 + i: i for i in range(len(outs))},
        compiler_params=PARAMS,
        cost_estimate=pl.CostEstimate(flops=20 * gradient.size, bytes_accessed=14 * gradient.size, transcendentals=0),
    )(at, gradient, first_moment, second_moment, *outs)


def body(inputs, dec_bias, weight, enc_bias, first_moment, second_moment):
    latents, width = weight.shape
    half = width // 2
    part = half // SIDE
    x, y, c = lax.axis_index("x"), lax.axis_index("y"), lax.axis_index("c")
    zh, z = lax.axis_index("zh"), lax.axis_index(Z)
    last_me, first_me = jnp.where(c == 0, x, y), jnp.where(c == 0, y, x)
    me = jnp.stack([c, last_me, first_me, z]).astype(jnp.int32)

    kept = lax.dynamic_slice_in_dim(inputs, c * half + x * part, part, 1)
    given = swap(lax.dynamic_slice_in_dim(inputs, (1 - c) * half + x * part, part, 1))
    both = jnp.concatenate([jnp.where(c == 0, kept, given), jnp.where(c == 0, given, kept)], 0)
    count = both.shape[0]
    block = lax.dynamic_update_slice_in_dim(jnp.zeros((SIDE * count, part), BF16), both, zh * count, 0)
    for by in ORDER[1:]:
        arrived = lax.ppermute(both, "zh", [(i, (i + by) % SIDE) for i in range(SIDE)])
        block = lax.dynamic_update_slice_in_dim(block, arrived, (zh - by) % SIDE * count, 0)
    source = block
    split = source.shape[0] // CHUNKS
    gathered = spread(source, False)

    pair = jnp.concatenate(
        [lax.dynamic_slice_in_dim(rows_held, c * half, half, 1) for rows_held in (weight, swap(weight))], 0
    )
    decoder = lax.dynamic_slice_in_dim(dec_bias, c * half, half, 0)[None, :]
    lift = jnp.concatenate([enc_bias, jnp.zeros_like(enc_bias)])[None, :]
    rows = source.shape[0] * SIDE
    thin = source.shape[0] // 8

    def fan(gathered, send):
        return [send(jnp.stack([g[k * split : (k + 1) * split] for g in gathered])) for k in chunks]

    chunks = range(CHUNKS)
    pieces = fan(gathered, relay)
    ahead, made = [], []
    for k in chunks:
        ahead.append(project(me, pair, decoder, lift, pieces[k], True))
        made.append(recon(me, ahead[k][1], swap(ahead[k][1]), pair, k > 0))
    blocks = jnp.concatenate([fold(*made[k][2:]) for k in chunks], 1)
    strip = blocks[0].astype(F32)
    for by in ORDER[1:]:
        strip = strip + shift(blocks[ORDER.index(SIDE - by)], by, False).astype(F32)
    parts = lax.all_to_all(strip.astype(BF16).reshape(8, thin, part), Z, 0, 0, tiled=True)
    error = find_error(me, parts, source, decoder)
    error = lax.all_to_all(error, Z, 0, 0, tiled=True)
    pieces = fan(spread(error.reshape(-1, part), False), lambda piece: spread(piece, True))
    total = None
    for k in chunks:
        after = () if total is None else (total,)
        laid, own = project(me, pair, decoder, lift, pieces[k], False, after, total is None)
        total = gradient((own, swap(own), made[k][0], made[k][1], laid, ahead[k][0]), total)
    mine, theirs = total
    arrived = swap(theirs)
    at = c.astype(jnp.int32)[None]
    outs = adam(at, mine, first_moment, second_moment, (), rows)
    return tuple(adam(1 - at, arrived, first_moment, second_moment, outs, rows))


def solution(mesh):
    fine = Mesh(mesh.devices.reshape(4, 2, 4, 4, 2), ("x", "zl", "y", "zh", "c"))
    lat = ("y", "zh", "c")
    everything = ("x", "zl", "y", "zh", "c")
    return jax.shard_map(
        body,
        mesh=fine,
        in_specs=(P(lat, None), P(), P(everything, None), P(everything), P(everything, None), P(everything, None)),
        out_specs=(P(everything, None),) * 3,
        check_vma=False,
    )
```
